512 devices in a mesh: dp: 64 (over x, z, core), tensor: 8 (over y).
Axes of the slice: x: 4, y: 8, z: 8, core: 2. Of those that a mesh axis runs over, the one named last changes fastest.
Arguments:
- tokens: bfloat16 [2, 4096, 8192], P(None, 'dp'), may hold values from -6 to 6
- value_matrix: bfloat16 [8192, 1024], P(None, 'tensor'), may hold values from -0.0625 to 0.0625
- adapter_down_weight: bfloat16 [256, 8192, 64], P('dp', 'tensor'), may hold values from -0.0625 to 0.0625
- adapter_up_weight: bfloat16 [256, 64, 1024], P('dp', None, 'tensor'), may hold values from -0.75 to 0.75
- adapter_index: int32 [2, 4096], P(None, 'dp'), may hold values from 0 to 255, as said below
Outputs:
- values: bfloat16 [2, 4096, 1024], P(None, 'dp', 'tensor')
The draws below stay inside these ranges and needn't reach their ends.
Inputs may be any that keep to these rules, and one draw needn't show every extreme that they name: `adapter_index`: adapter a is owned by dp shard a // 4. Of the 64 rows of one dp shard in one group, at most 2 use adapters of one owner, and in each group one owner takes exactly 2 rows from every dp shard.
All inputs are finite; a program needn't handle non-finite values.
Results may differ from the reference program's by a relative error of at most 0.0038.
Values may be sent and summed in bfloat16 or wider, within the bound.
No kernel may reach another device: no remote copies, remote signals or barrier semaphores. Data moves between devices by JAX's collectives and lax.ppermute only.
A program may use at most 64 MiB of HBM per device.

```python
import jax
import jax.numpy as jnp
from jax import lax

MODEL_WIDTH = 8192
KEY_VALUE_HEADS = 8
HEAD_SIZE = 128
ADAPTER_RANK = 64
DECODE_GROUPS = 2
ROWS_DEV = 64
ADAPT_DEV = 4
GROUP_ROWS = 4096
ADAPTER_POOL = 256
CAP = 2
N_DP = 64


def draw_adapter_index(key, part):
    key = jax.random.fold_in(key, 11)
    hot_key, other_key, shuffle_key, local_key = jax.random.split(key, 4)
    hot_owner = jax.random.randint(hot_key, (DECODE_GROUPS,), 0, N_DP).astype(jnp.int32)
    other_keys = jax.random.split(other_key, DECODE_GROUPS * N_DP)
    others = jax.vmap(lambda single: jax.random.permutation(single, N_DP - 1))(other_keys)
    others = others.reshape(DECODE_GROUPS, N_DP, N_DP - 1).astype(jnp.int32)
    others = others + (others >= hot_owner[:, None, None]).astype(jnp.int32)
    position = jnp.arange(ROWS_DEV, dtype=jnp.int32)
    pick = jnp.maximum(position - CAP, 0) // CAP % (N_DP - 1)
    owners = jnp.where(position[None, None, :] < CAP, hot_owner[:, None, None], jnp.take(others, pick, axis=2))
    shuffle_keys = jax.random.split(shuffle_key, DECODE_GROUPS * N_DP)
    shuffle = jax.vmap(lambda single: jax.random.permutation(single, ROWS_DEV))(shuffle_keys)
    shuffle = shuffle.reshape(DECODE_GROUPS, N_DP, ROWS_DEV).astype(jnp.int32)
    owners = jnp.take_along_axis(owners, shuffle, axis=2)
    local = jax.random.randint(local_key, (DECODE_GROUPS, N_DP, ROWS_DEV), 0, ADAPT_DEV).astype(jnp.int32)
    return (owners * ADAPT_DEV + local).reshape(DECODE_GROUPS, GROUP_ROWS).astype(jnp.int32)


def steps_of(key, dims, cuts, low, high):
    factor_of, own = 1.0, jax.random.fold_in(key, 6)
    for dim, parts in cuts:
        heights = jnp.exp(jax.random.uniform(jax.random.fold_in(own, dim), (parts,), jnp.float32, low / len(cuts), high / len(cuts)))
        factor_of = factor_of * jnp.repeat(heights, dims[dim] // parts).reshape([-1 if axis == dim else 1 for axis in range(len(dims))])
    return factor_of


def noise(key, extent, deviation, limit, shards=(), kind=jnp.bfloat16):
    drawn = deviation * jax.random.normal(key, extent, jnp.float32)
    if shards:
        drawn = drawn * steps_of(key, extent, shards, -0.22, 0.18)
    return jnp.clip(drawn, -limit, limit).astype(kind)


def setup_inputs(seed: int = 0) -> dict:
    splits = jax.random.split(jax.random.key(seed), 6)
    tokens = noise(splits[0], (DECODE_GROUPS, GROUP_ROWS, MODEL_WIDTH), 1.0, 6.0, ((1, 64),))
    value_matrix = noise(splits[1], (MODEL_WIDTH, KEY_VALUE_HEADS * HEAD_SIZE), MODEL_WIDTH ** -0.5, 0.0625, ((1, 8),))
    adapter_down_weight = noise(splits[2], (ADAPTER_POOL, MODEL_WIDTH, ADAPTER_RANK), MODEL_WIDTH ** -0.5, 0.0625, ((0, 64), (1, 8)))
    adapter_up_weight = noise(splits[3], (ADAPTER_POOL, ADAPTER_RANK, KEY_VALUE_HEADS * HEAD_SIZE), ADAPTER_RANK ** -0.5, 0.75, ((0, 64), (2, 8)))
    adapter_index = draw_adapter_index(jax.random.fold_in(splits[5], 71), 0)
    return {"tokens": tokens, "value_matrix": value_matrix, "adapter_down_weight": adapter_down_weight, "adapter_up_weight": adapter_up_weight, "adapter_index": adapter_index}


def reference(tokens, value_matrix, adapter_down_weight, adapter_up_weight, adapter_index):
    flat_tokens = tokens.reshape(DECODE_GROUPS * GROUP_ROWS, MODEL_WIDTH)
    base_output = jnp.dot(flat_tokens, value_matrix, preferred_element_type=jnp.float32)
    block_rows = 8
    blocks = (DECODE_GROUPS * GROUP_ROWS) // block_rows
    token_block_rows = flat_tokens.reshape(blocks, block_rows, MODEL_WIDTH)
    index_blocks = adapter_index.reshape(blocks, block_rows).astype(jnp.int32)

    def single_block(pair):
        block_tokens, block_index = pair
        down_weight_rows = adapter_down_weight[block_index].astype(jnp.float32)
        shrunk_output = jnp.einsum("rd,rdk->rk", block_tokens.astype(jnp.float32), down_weight_rows, precision=lax.Precision.HIGHEST)
        shrunk_output = shrunk_output.astype(jnp.bfloat16)
        up_weight_rows = adapter_up_weight[block_index].astype(jnp.float32)
        return jnp.einsum("rk,rkc->rc", shrunk_output.astype(jnp.float32), up_weight_rows, precision=lax.Precision.HIGHEST)

    adapter_output = lax.map(single_block, (token_block_rows, index_blocks)).reshape(DECODE_GROUPS * GROUP_ROWS, KEY_VALUE_HEADS * HEAD_SIZE)
    values = (base_output + adapter_output).astype(jnp.bfloat16)
    return values.reshape(DECODE_GROUPS, GROUP_ROWS, KEY_VALUE_HEADS * HEAD_SIZE)
```

```python
import functools

import jax
import jax.numpy as jnp
from jax import lax
from jax.experimental import pallas as pl
from jax.experimental.pallas import tpu as pltpu
from jax.sharding import PartitionSpec as P

BF16, F32, I32 = jnp.bfloat16, jnp.float32, jnp.int32
VMEM_LIMIT = 40 * 1024 * 1024


def iota(shape, dim):
    return lax.broadcasted_iota(I32, shape, dim)


def slots_of(index_row, owned, slots):
    rows = index_row.shape[1]
    wide = jnp.broadcast_to(index_row, (rows, rows))
    line, column = iota((rows, rows), 0), iota((rows, rows), 1)
    index_col = jnp.sum(jnp.where(line == column, wide, 0), axis=1, keepdims=True)
    half = rows // 2
    same_group = (line >= half) == (column >= half)
    same = (wide // owned == index_col // owned) & same_group
    before = jnp.sum(jnp.where(same & (line < column), 1, 0), axis=0, keepdims=True)
    before_col = jnp.sum(jnp.where(same & (column < line), 1, 0), axis=1, keepdims=True)
    group_row = jnp.where(iota((1, rows), 1) >= half, 2, 0)
    group_col = jnp.where(iota((rows, 1), 0) >= half, 2, 0)
    return group_row + before, group_col + before_col, index_col


def pack_kernel(owned, owners, index_ref, tokens_ref, out_ref, held, sem):
    width = held.shape[2]
    start = pl.multiple_of(lax.axis_index("tensor") * width, width)
    copy = pltpu.make_async_copy(tokens_ref.at[:, :, pl.ds(start, width)], held, sem)
    copy.start()
    index_row = index_ref[...]
    rows = index_row.shape[1]
    slot, _, index_col = slots_of(index_row, owned, 4)
    target = index_row // owned * 8 + slot
    both = jnp.concatenate([target, target + 4], axis=1)
    lines = owners * 8
    select = jnp.where(iota((lines, 2 * rows), 0) == both, 1.0, 0.0).astype(BF16)
    label = jnp.broadcast_to((index_col % owned + 1).astype(F32), (rows, 128)).astype(BF16)
    labels = jnp.concatenate([label, label], axis=0)
    half = width // 2
    out_ref[:, half:] = jnp.dot(select, labels, preferred_element_type=F32).astype(BF16)
    copy.wait()
    tokens = held[...].reshape(rows, width)
    halves = jnp.concatenate([tokens[:, :half], tokens[:, half:]], axis=0)
    out_ref[:, :half] = jnp.dot(select, halves, preferred_element_type=F32).astype(BF16)


def pair_up(lines):
    by_shard = lines.reshape(2, lines.shape[0] // 32, 2, 8, 128)
    low = iota((lines.shape[0] // 32, 8, 128), 1) < 4
    return [
        jnp.where(low, by_shard[e, :, 0], by_shard[e, :, 1]).reshape(lines.shape[0] // 4, 128)
        for e in range(2)
    ]


def shrink_kernel(received_ref, down_ref, partial_ref, label_ref):
    lines = received_ref.shape[0]
    half = down_ref.shape[0]
    product = jnp.dot(received_ref[:, :half], down_ref[...], preferred_element_type=F32)
    label = received_ref[:, half:].astype(F32)
    second = iota((lines, 128), 0) % 8 >= 4
    upper = iota((lines, 128), 1) >= 64
    left = jnp.where(second, product[:, 256:384], product[:, :128])
    right = jnp.where(second, product[:, 384:], product[:, 128:256])
    total = jnp.where(label == jnp.where(upper, 2.0, 1.0), left, 0.0) + jnp.where(
        label == jnp.where(upper, 4.0, 3.0), right, 0.0
    )
    total = total + pltpu.roll(total, 64, 1)
    by_shard = total.reshape(lines // 8, 8, 128)
    total = (by_shard + pltpu.roll(by_shard, 4, 1)).reshape(lines, 128)
    first, last = pair_up(total)
    packed = jnp.where(iota(first.shape, 1) < 64, first, last).astype(BF16)
    for peer in range(partial_ref.shape[0]):
        partial_ref[peer] = packed
    labels = pair_up(label)
    for e in range(2):
        label_ref[e] = labels[e].astype(BF16)


def expand_kernel(partial_ref, label_ref, up_ref, out_ref):
    total = partial_ref[0].astype(F32)
    for peer in range(1, partial_ref.shape[0]):
        total = total + partial_ref[peer].astype(F32)
    turned = pltpu.roll(total, 64, 1)
    upper = iota(total.shape, 1) >= 64
    lines = total.shape[0]
    for e in range(2):
        row = jnp.where(upper, turned, total) if e == 0 else jnp.where(upper, total, turned)
        label = label_ref[e].astype(F32)
        left = jnp.where(label == jnp.where(upper, 2.0, 1.0), row, 0.0)
        right = jnp.where(label == jnp.where(upper, 4.0, 3.0), row, 0.0)
        wide = jnp.concatenate([left, right], axis=1).astype(BF16)
        out_ref[e * lines : (e + 1) * lines] = jnp.dot(
            wide, up_ref[...], preferred_element_type=F32
        )


def place_kernel(owned, owners, index_ref, out_ref):
    index_row = index_ref[...]
    rows = index_row.shape[1]
    _, slot, index_col = slots_of(index_row, owned, 4)
    target = index_col // owned * 4 + slot
    out_ref[...] = jnp.where(iota((rows, owners * 4), 1) == target, 1.0, 0.0).astype(BF16)


def add_kernel(place_ref, arrived_ref, base_ref, out_ref):
    arrived = arrived_ref[...]
    high = arrived.astype(BF16)
    low = (arrived - high.astype(F32)).astype(BF16)
    place = place_ref[...]
    terms = jnp.dot(place, high, preferred_element_type=F32) + jnp.dot(
        place, low, preferred_element_type=F32
    )
    out_ref[...] = (base_ref[...] + terms).astype(BF16)


def call(kernel, shapes, ins, scratch=(), flops=0, any_at=()):
    nbytes = sum(v.size * v.dtype.itemsize for v in ins)
    return pl.pallas_call(
        kernel,
        out_shape=shapes,
        in_specs=[
            pl.BlockSpec(memory_space=pl.ANY if i in any_at else pltpu.VMEM)
            for i in range(len(ins))
        ],
        out_specs=jax.tree.map(lambda _: pl.BlockSpec(memory_space=pltpu.VMEM), shapes),
        scratch_shapes=scratch,
        compiler_params=pltpu.CompilerParams(vmem_limit_bytes=VMEM_LIMIT),
        cost_estimate=pl.CostEstimate(flops=flops, bytes_accessed=nbytes, transcendentals=0),
    )(*ins)


def on_device(tokens, value_matrix, down, up, index):
    groups, rows_local, features = tokens.shape
    owners = lax.axis_size("dp")
    planes = lax.axis_size("tensor")
    owned, width, rank = down.shape
    columns = up.shape[2]
    rows = groups * rows_local
    half = width // 2
    lines = owners * 8
    shape = jax.ShapeDtypeStruct
    index_row = index.reshape(1, rows)

    packed = call(
        functools.partial(pack_kernel, owned, owners),
        shape((lines, half + 128), BF16),
        (index_row, tokens),
        [pltpu.VMEM((groups, rows_local, width), BF16), pltpu.SemaphoreType.DMA],
        any_at=(1,),
    )
    received = lax.all_to_all(
        packed.reshape(owners, 8, half + 128), "dp", split_axis=0, concat_axis=0, tiled=True
    ).reshape(lines, half + 128)

    base = jnp.dot(
        tokens.reshape(rows, features), value_matrix, preferred_element_type=F32
    )
    place = call(
        functools.partial(place_kernel, owned, owners),
        shape((rows, owners * 4), BF16),
        (index_row,),
    )
    down_wide = down.reshape(owned, 2, half, rank).transpose(2, 1, 0, 3).reshape(half, -1)

    partial, label = call(
        shrink_kernel,
        (shape((planes, lines // 4, 128), BF16), shape((2, lines // 4, 128), BF16)),
        (received, down_wide),
    )
    partials = lax.all_to_all(partial, "tensor", split_axis=0, concat_axis=0, tiled=True)
    terms = call(
        expand_kernel,
        shape((owners * 4, columns), F32),
        (partials, label, up.reshape(owned * rank, columns)),
    )
    arrived = lax.all_to_all(
        terms.reshape(owners, 4, columns), "dp", split_axis=0, concat_axis=0, tiled=True
    ).reshape(owners * 4, columns)
    out = call(add_kernel, shape((rows, columns), BF16), (place, arrived, base))
    return out.reshape(groups, rows_local, columns)


def solution(mesh):
    in_specs = (
        P(None, "dp", None),
        P(None, "tensor"),
        P("dp", "tensor", None),
        P("dp", None, "tensor"),
        P(None, "dp"),
    )
    out_specs = P(None, "dp", "tensor")
    return jax.shard_map(
        on_device, mesh=mesh, in_specs=in_specs, out_specs=out_specs, check_vma=False
    )
```

```python
import functools

import jax
import jax.numpy as jnp
from jax import lax
from jax.experimental import pallas as pl
from jax.experimental.pallas import tpu as pltpu
from jax.sharding import PartitionSpec as P

BF16, F32, I32 = jnp.bfloat16, jnp.float32, jnp.int32
MIB = 1024 * 1024


def iota(shape, dim):
    return lax.broadcasted_iota(I32, shape, dim)


def read_index(index_ref, owned):
    along = jnp.concatenate([index_ref[0:1, :], index_ref[1:2, :]], axis=1)
    rows = along.shape[1]
    wide = jnp.broadcast_to(along, (rows, rows))
    line, column = iota((rows, rows), 0), iota((rows, rows), 1)
    down = jnp.sum(jnp.where(line == column, wide, 0), axis=1, keepdims=True)
    half = rows // 2
    same = (wide // owned == down // owned) & ((line >= half) == (column >= half))
    place = jnp.sum(jnp.where(same & (line < column), 1, 0), axis=0, keepdims=True)
    place_down = jnp.sum(jnp.where(same & (column < line), 1, 0), axis=1, keepdims=True)
    group = jnp.where(iota((1, rows), 1) >= half, 1, 0)
    group_down = jnp.where(iota((rows, 1), 0) >= half, 1, 0)
    return (along, place, group), (down, place_down, group_down)


def pack_kernel(owned, owners, index_ref, tokens_ref, out_ref, held, sems):
    quarter = held.shape[3]
    plane = lax.axis_index("tensor")
    parity = plane % 2
    copies = []
    for e in range(4):
        from_plane = plane if e < 2 else plane + 1 - 2 * parity
        start = pl.multiple_of(from_plane * (2 * quarter) + (e % 2) * quarter, quarter)
        copies.append(
            pltpu.make_async_copy(
                tokens_ref.at[:, :, pl.ds(start, quarter)], held.at[e], sems.at[e]
            )
        )
        copies[-1].start()
    (along, place, group), (down, _, _) = read_index(index_ref, owned)
    rows = along.shape[1]
    lines = owners * 8
    owner = along // owned
    first = jnp.where(place == parity, owner * 8 + group, -1)
    target = jnp.concatenate([jnp.where(first >= 0, first + 2 * e, -1) for e in range(4)], axis=1)
    select = jnp.where(iota((lines, 4 * rows), 0) == target, 1.0, 0.0).astype(BF16)
    wanted = owner * 2 + group
    wanted = jnp.concatenate([jnp.where(place == p, wanted, -1) for p in range(2)], axis=1)
    line = iota((lines, 2 * rows), 0)
    choose = jnp.where(line // 8 * 2 + line % 2 == wanted, 1.0, 0.0).astype(BF16)
    label = jnp.broadcast_to((down % owned + 1).astype(F32), (rows, 128))
    upper = iota((rows, 128), 1) >= 64
    labels = jnp.concatenate(
        [jnp.where(upper, 0.0, label), jnp.where(upper, label, 0.0)], axis=0
    ).astype(BF16)
    out_ref[:, quarter:] = jnp.dot(choose, labels, preferred_element_type=F32).astype(BF16)
    for copy in copies:
        copy.wait()
    tokens = held[...].reshape(4 * rows, quarter)
    out_ref[:, :quarter] = jnp.dot(select, tokens, preferred_element_type=F32).astype(BF16)


def shrink_kernel(received_ref, own_ref, other_ref, partial_ref, label_ref):
    lines = received_ref.shape[0]
    quarter = received_ref.shape[1] - 128
    shards = lines // 8
    parity = lax.axis_index("tensor") % 2
    rows = received_ref[:, :quarter]
    part = iota((lines, 256), 0) % 8 // 2
    product = None
    for e in range(4):
        held = own_ref if e < 2 else other_ref
        weight = held[:, :, (e % 2) * quarter : (e % 2 + 1) * quarter].reshape(256, quarter)
        mine = lax.dot_general(
            rows, weight, (((1,), (1,)), ((), ())), preferred_element_type=F32
        )
        product = mine if e == 0 else jnp.where(part == e, mine, product)
    label = received_ref[:, quarter:].astype(F32)
    turned = pltpu.roll(label, 64, 1)
    upper = iota((lines, 128), 1) // 64
    here = jnp.where(upper == parity, label, turned)
    total = jnp.where(here == upper.astype(F32) + 1.0, product[:, :128], 0.0)
    total = total + jnp.where(here == upper.astype(F32) + 3.0, product[:, 128:], 0.0)
    total = (total + pltpu.roll(total, 64, 1)).reshape(shards, 8, 128)
    total = total + pltpu.roll(total, 4, 1)
    total = total + pltpu.roll(total, 2, 1)
    by_shard = total.reshape(2, shards // 8, 4, 8, 128)
    pair = iota((shards // 8, 8, 128), 1) // 2
    halves = []
    for e in range(2):
        chosen = by_shard[e, :, 0]
        for d in range(1, 4):
            chosen = jnp.where(pair == d, by_shard[e, :, d], chosen)
        halves.append(chosen)
    packed = jnp.where(iota((shards // 8, 8, 128), 2) < 64, halves[0], halves[1])
    packed = packed.reshape(shards, 128).astype(BF16)
    for peer in range(partial_ref.shape[0]):
        partial_ref[peer] = packed
    low = jnp.where(upper == 0, label, turned)
    high = jnp.where(upper == 0, turned, label)
    place = iota((lines, 128), 0) // 2 % 2
    both = jnp.where(place == 0, low, high).reshape(2, shards // 4, 2, 8, 128)
    even = iota((shards // 4, 8, 128), 1) < 4
    for e in range(2):
        chosen = jnp.where(even, both[e, :, 0], both[e, :, 1])
        label_ref[e] = chosen.reshape(shards * 2, 128).astype(BF16)


def expand_kernel(partial_ref, label_ref, up_ref, out_ref):
    planes, shards, _ = partial_ref.shape
    sums = []
    for p in range(2):
        total = partial_ref[p].astype(F32)
        for peer in range(p + 2, planes, 2):
            total = total + partial_ref[peer].astype(F32)
        sums.append(total.reshape(shards // 8, 8, 128))
    first, second = sums
    pair = iota(first.shape, 1) // 2

    def spread(pieces):
        out = pieces[0]
        for d in range(1, 4):
            out = jnp.where(pair == d, pieces[d], out)
        return out

    def turn(total, by):
        return pltpu.roll(total, by, 1)

    even = spread([first, turn(second, 2), turn(first, 2), turn(second, 4)])
    odd = spread([turn(first, 4), turn(second, 6), turn(first, 6), second])
    total = jnp.stack([even, odd], axis=1).reshape(shards * 2, 128)
    turned = pltpu.roll(total, 64, 1)
    upper = iota(total.shape, 1) // 64
    lines = total.shape[0]
    for e in range(2):
        row = jnp.where(upper == e, total, turned)
        label = label_ref[e].astype(F32)
        left = jnp.where(label == upper.astype(F32) + 1.0, row, 0.0)
        right = jnp.where(label == upper.astype(F32) + 3.0, row, 0.0)
        wide = jnp.concatenate([left, right], axis=1).astype(BF16)
        out_ref[e * lines : (e + 1) * lines] = jnp.dot(
            wide, up_ref[...], preferred_element_type=F32
        )


def place_kernel(owned, owners, index_ref, out_ref):
    _, (down, place, group) = read_index(index_ref, owned)
    target = down // owned * 4 + place * 2 + group
    out_ref[...] = jnp.where(iota(out_ref.shape, 1) == target, 1.0, 0.0).astype(BF16)


def add_kernel(place_ref, arrived_ref, base_ref, out_ref):
    arrived = arrived_ref[...]
    high = arrived.astype(BF16)
    low = (arrived - high.astype(F32)).astype(BF16)
    place = place_ref[...]
    terms = jnp.dot(place, high, preferred_element_type=F32) + jnp.dot(
        place, low, preferred_element_type=F32
    )
    out_ref[...] = (base_ref[...] + terms).astype(BF16)


def call(kernel, shapes, ins, scratch=(), flops=0, in_hbm=(), vmem=40):
    nbytes = sum(v.size * v.dtype.itemsize for v in ins)
    return pl.pallas_call(
        kernel,
        out_shape=shapes,
        in_specs=[
            pl.BlockSpec(memory_space=pltpu.HBM if i in in_hbm else pltpu.VMEM)
            for i in range(len(ins))
        ],
        out_specs=jax.tree.map(lambda _: pl.BlockSpec(memory_space=pltpu.VMEM), shapes),
        scratch_shapes=scratch,
        compiler_params=pltpu.CompilerParams(vmem_limit_bytes=vmem * MIB),
        cost_estimate=pl.CostEstimate(flops=flops, bytes_accessed=nbytes, transcendentals=0),
    )(*ins)


def on_device(tokens, value_matrix, down, up, index):
    groups, rows_local, features = tokens.shape
    owners = lax.axis_size("dp")
    planes = lax.axis_size("tensor")
    owned, width, rank = down.shape
    columns = up.shape[2]
    rows = groups * rows_local
    quarter = width // 2
    lines = owners * 8
    shape = jax.ShapeDtypeStruct

    packed = call(
        functools.partial(pack_kernel, owned, owners),
        shape((lines, quarter + 128), BF16),
        (index, tokens),
        [pltpu.VMEM((4, groups, rows_local, quarter), BF16), pltpu.SemaphoreType.DMA((4,))],
        in_hbm=(1,),
        vmem=62,
    )
    received = lax.all_to_all(
        packed.reshape(owners, 8, quarter + 128), "dp", split_axis=0, concat_axis=0, tiled=True
    ).reshape(lines, quarter + 128)

    down_own = down.transpose(0, 2, 1)
    sent_first, _ = lax.optimization_barrier((down_own, packed))
    down_other = lax.ppermute(sent_first, "tensor", [(i, i ^ 1) for i in range(planes)])
    base = jnp.dot(tokens.reshape(rows, features), value_matrix, preferred_element_type=F32)
    place = call(
        functools.partial(place_kernel, owned, owners), shape((rows, owners * 4), BF16), (index,)
    )

    partial, label = call(
        shrink_kernel,
        (shape((planes, owners, 128), BF16), shape((2, owners * 2, 128), BF16)),
        (received, down_own, down_other),
    )
    partials = lax.all_to_all(partial, "tensor", split_axis=0, concat_axis=0, tiled=True)
    terms = call(
        expand_kernel,
        shape((owners * 4, columns), F32),
        (partials, label, up.reshape(owned * rank, columns)),
    )
    arrived = lax.all_to_all(
        terms.reshape(owners, 4, columns), "dp", split_axis=0, concat_axis=0, tiled=True
    ).reshape(owners * 4, columns)
    out = call(add_kernel, shape((rows, columns), BF16), (place, arrived, base))
    return out.reshape(groups, rows_local, columns)


def solution(mesh):
    in_specs = (
        P(None, "dp", None),
        P(None, "tensor"),
        P("dp", "tensor", None),
        P("dp", None, "tensor"),
        P(None, "dp"),
    )
    out_specs = P(None, "dp", "tensor")
    return jax.shard_map(
        on_device, mesh=mesh, in_specs=in_specs, out_specs=out_specs, check_vma=False
    )
```

```python
import functools

import jax
import jax.numpy as jnp
from jax import lax
from jax.experimental import pallas as pl
from jax.experimental.pallas import tpu as pltpu
from jax.sharding import PartitionSpec as P

BF16, F32, I32 = jnp.bfloat16, jnp.float32, jnp.int32
MIB = 1024 * 1024


def iota(shape, dim):
    return lax.broadcasted_iota(I32, shape, dim)


def read_index(index_ref, owned):
    along = jnp.concatenate([index_ref[0:1, :], index_ref[1:2, :]], axis=1)
    rows = along.shape[1]
    wide = jnp.broadcast_to(along, (rows, rows))
    line, column = iota((rows, rows), 0), iota((rows, rows), 1)
    down = jnp.sum(jnp.where(line == column, wide, 0), axis=1, keepdims=True)
    half = rows // 2
    same = (wide // owned == down // owned) & ((line >= half) == (column >= half))
    place = jnp.sum(jnp.where(same & (line < column), 1, 0), axis=0, keepdims=True)
    place_down = jnp.sum(jnp.where(same & (column < line), 1, 0), axis=1, keepdims=True)
    group = jnp.where(iota((1, rows), 1) >= half, 1, 0)
    group_down = jnp.where(iota((rows, 1), 0) >= half, 1, 0)
    return (along, place, group), (down, place_down, group_down)


def spread(first, second):
    first, second = (v.reshape(v.shape[0] // 8, 8, 128) for v in (first, second))
    pair = iota(first.shape, 1) // 2

    def turn(total, by):
        return pltpu.roll(total, by, 1)

    def pick(*pieces):
        out = pieces[0]
        for d in range(1, 4):
            out = jnp.where(pair == d, pieces[d], out)
        return out

    even = pick(first, turn(second, 2), turn(first, 2), turn(second, 4))
    odd = pick(turn(first, 4), turn(second, 6), turn(first, 6), second)
    return jnp.stack([even, odd], axis=1).reshape(first.shape[0] * 16, 128)


def pack_kernel(owned, owners, index_ref, tokens_ref, out_ref, held, sems):
    width = held.shape[2] // 2
    plane = lax.axis_index("tensor")
    parity = plane % 2
    copies = []
    for e in range(2):
        from_plane = plane if e == 0 else plane + 1 - 2 * parity
        start = pl.multiple_of(from_plane * width, width)
        copies.append(
            pltpu.make_async_copy(
                tokens_ref.at[:, :, pl.ds(start, width)],
                held.at[:, :, e * width : (e + 1) * width],
                sems.at[e],
            )
        )
        copies[-1].start()
    (along, place, group), (down, _, _) = read_index(index_ref, owned)
    rows = along.shape[1]
    lines = owners * 2
    wanted = along // owned * 2 + group
    select = jnp.where(
        (iota((lines, rows), 0) == wanted) & (place == parity), 1.0, 0.0
    ).astype(BF16)
    both = jnp.concatenate([jnp.where(place == p, wanted, -1) for p in range(2)], axis=1)
    choose = jnp.where(iota((lines, 2 * rows), 0) == both, 1.0, 0.0).astype(BF16)
    label = jnp.broadcast_to((down % owned + 1).astype(F32), (rows, 128))
    upper = iota((rows, 128), 1) >= 64
    labels = jnp.concatenate(
        [jnp.where(upper, 0.0, label), jnp.where(upper, label, 0.0)], axis=0
    ).astype(BF16)
    labels = jnp.dot(choose, labels, preferred_element_type=F32).astype(BF16)
    out_ref[:, :, 2 * width :] = labels.reshape(owners, 2, 128)
    for copy in copies:
        copy.wait()
    tokens = held[...].reshape(rows, 2 * width)
    packed = jnp.dot(select, tokens, preferred_element_type=F32).astype(BF16)
    out_ref[:, :, : 2 * width] = packed.reshape(owners, 2, 2 * width)


def shrink_kernel(received_ref, own_ref, other_ref, partial_ref, label_ref):
    shards, groups, width = received_ref.shape
    width = (width - 128) // 2
    lines = shards * groups
    parity = lax.axis_index("tensor") % 2
    product = None
    for e in range(2):
        rows = received_ref[:, :, e * width : (e + 1) * width].reshape(lines, width)
        weight = (own_ref if e == 0 else other_ref)[...].reshape(256, width)
        mine = lax.dot_general(
            rows, weight, (((1,), (1,)), ((), ())), preferred_element_type=F32
        )
        product = mine if e == 0 else product + mine
    label = received_ref[:, :, 2 * width :].reshape(lines, 128).astype(F32)
    turned = pltpu.roll(label, 64, 1)
    upper = iota((lines, 128), 1) // 64
    here = jnp.where(upper == parity, label, turned)
    total = jnp.where(here == upper.astype(F32) + 1.0, product[:, :128], 0.0)
    total = total + jnp.where(here == upper.astype(F32) + 3.0, product[:, 128:], 0.0)
    total = total + pltpu.roll(total, 64, 1)
    half = lines // 2
    packed = jnp.where(upper[:half] == 0, total[:half], total[half:]).astype(BF16)
    for peer in range(partial_ref.shape[0]):
        partial_ref[peer] = packed
    low = jnp.where(upper == 0, label, turned)
    high = jnp.where(upper == 0, turned, label)
    label_ref[...] = spread(low, high).astype(BF16)


def expand_kernel(partial_ref, label_ref, up_ref, out_ref):
    sums = []
    for p in range(2):
        total = partial_ref[p].astype(F32)
        for peer in range(p + 2, partial_ref.shape[0], 2):
            total = total + partial_ref[peer].astype(F32)
        sums.append(total)
    total = spread(*sums)
    turned = pltpu.roll(total, 64, 1)
    upper = iota(total.shape, 1) // 64
    lines = total.shape[0]
    for e in range(2):
        row = jnp.where(upper == e, total, turned)
        label = label_ref[e * lines : (e + 1) * lines].astype(F32)
        left = jnp.where(label == upper.astype(F32) + 1.0, row, 0.0)
        right = jnp.where(label == upper.astype(F32) + 3.0, row, 0.0)
        wide = jnp.concatenate([left, right], axis=1).astype(BF16)
        out_ref[e * lines : (e + 1) * lines] = jnp.dot(
            wide, up_ref[...], preferred_element_type=F32
        )


def place_kernel(owned, owners, index_ref, out_ref):
    _, (down, place, group) = read_index(index_ref, owned)
    target = down // owned * 4 + place * 2 + group
    out_ref[...] = jnp.where(iota(out_ref.shape, 1) == target, 1.0, 0.0).astype(BF16)


def add_kernel(place_ref, arrived_ref, base_ref, out_ref):
    arrived = arrived_ref[...]
    high = arrived.astype(BF16)
    low = (arrived - high.astype(F32)).astype(BF16)
    place = place_ref[...]
    terms = jnp.dot(place, high, preferred_element_type=F32) + jnp.dot(
        place, low, preferred_element_type=F32
    )
    out_ref[...] = (base_ref[...] + terms).astype(BF16)


def call(kernel, shapes, ins, scratch=(), flops=0, in_hbm=(), vmem=40):
    nbytes = sum(v.size * v.dtype.itemsize for v in ins)
    return pl.pallas_call(
        kernel,
        out_shape=shapes,
        in_specs=[
            pl.BlockSpec(memory_space=pltpu.HBM if i in in_hbm else pltpu.VMEM)
            for i in range(len(ins))
        ],
        out_specs=jax.tree.map(lambda _: pl.BlockSpec(memory_space=pltpu.VMEM), shapes),
        scratch_shapes=scratch,
        compiler_params=pltpu.CompilerParams(vmem_limit_bytes=vmem * MIB),
        cost_estimate=pl.CostEstimate(flops=flops, bytes_accessed=nbytes, transcendentals=0),
    )(*ins)


def on_device(tokens, value_matrix, down, up, index):
    groups, rows_local, features = tokens.shape
    owners = lax.axis_size("dp")
    planes = lax.axis_size("tensor")
    owned, width, rank = down.shape
    columns = up.shape[2]
    rows = groups * rows_local
    shape = jax.ShapeDtypeStruct

    packed = call(
        functools.partial(pack_kernel, owned, owners),
        shape((owners, groups, 2 * width + 128), BF16),
        (index, tokens),
        [pltpu.VMEM((groups, rows_local, 2 * width), BF16), pltpu.SemaphoreType.DMA((2,))],
        in_hbm=(1,),
        vmem=62,
    )
    received = lax.all_to_all(packed, "dp", split_axis=0, concat_axis=0, tiled=True)

    down_own = down.transpose(0, 2, 1)
    sent_first, _ = lax.optimization_barrier((down_own, packed))
    down_other = lax.ppermute(sent_first, "tensor", [(i, i ^ 1) for i in range(planes)])
    base = jnp.dot(tokens.reshape(rows, features), value_matrix, preferred_element_type=F32)
    place = call(
        functools.partial(place_kernel, owned, owners), shape((rows, owners * 4), BF16), (index,)
    )

    partial, label = call(
        shrink_kernel,
        (shape((planes, owners, 128), BF16), shape((owners * 4, 128), BF16)),
        (received, down_own, down_other),
    )
    partials = lax.all_to_all(partial, "tensor", split_axis=0, concat_axis=0, tiled=True)
    terms = call(
        expand_kernel,
        shape((owners * 4, columns), F32),
        (partials, label, up.reshape(owned * rank, columns)),
    )
    arrived = lax.all_to_all(
        terms.reshape(owners, 4, columns), "dp", split_axis=0, concat_axis=0, tiled=True
    ).reshape(owners * 4, columns)
    out = call(add_kernel, shape((rows, columns), BF16), (place, arrived, base))
    return out.reshape(groups, rows_local, columns)


def solution(mesh):
    in_specs = (
        P(None, "dp", None),
        P(None, "tensor"),
        P("dp", "tensor", None),
        P("dp", None, "tensor"),
        P(None, "dp"),
    )
    out_specs = P(None, "dp", "tensor")
    return jax.shard_map(
        on_device, mesh=mesh, in_specs=in_specs, out_specs=out_specs, check_vma=False
    )
```

```python
import functools

import jax
import jax.numpy as jnp
from jax import lax
from jax.experimental import pallas as pl
from jax.experimental.pallas import tpu as pltpu
from jax.sharding import PartitionSpec as P

BF16, F32, I32 = jnp.bfloat16, jnp.float32, jnp.int32
MIB = 1024 * 1024


def iota(shape, dim):
    return lax.broadcasted_iota(I32, shape, dim)


def read_index(index_ref, owned):
    along = jnp.concatenate([index_ref[0:1, :], index_ref[1:2, :]], axis=1)
    rows = along.shape[1]
    shift = owned.bit_length() - 1
    assert owned == 1 << shift
    key = (along >> shift) * 2 + jnp.where(iota((1, rows), 1) >= rows // 2, 1, 0)
    wide = jnp.broadcast_to(key, (rows, rows))
    line, column = iota((rows, rows), 0), iota((rows, rows), 1)
    same = jnp.sum(jnp.where(line == column, wide, 0).astype(F32), axis=1, keepdims=True)
    earlier = (wide.astype(F32) == same) & (line < column)
    place = jnp.sum(jnp.where(earlier, 1.0, 0.0), axis=0, keepdims=True)
    return wide, place, ((along & (owned - 1)) + 1).astype(F32)


def spread(first, second):
    first, second = (v.reshape(v.shape[0] // 8, 8, 128) for v in (first, second))
    pair = iota(first.shape, 1) // 2

    def turn(total, by):
        return pltpu.roll(total, by, 1)

    def pick(*pieces):
        out = pieces[0]
        for d in range(1, 4):
            out = jnp.where(pair == d, pieces[d], out)
        return out

    even = pick(first, turn(second, 2), turn(first, 2), turn(second, 4))
    odd = pick(turn(first, 4), turn(second, 6), turn(first, 6), second)
    return jnp.stack([even, odd], axis=1).reshape(first.shape[0] * 16, 128)


def pack_kernel(
    owned, planes, index_ref, tokens_ref, down_ref, out_ref, lower_ref, upper_ref, held, indices, sems
):
    width = down_ref.shape[2]
    half = width // 2
    features = planes * width
    plane = lax.axis_index("tensor")
    parity = plane % 2
    starts = [(plane * width + features - half) % features, plane * width]
    starts.append((plane * width + width) % features)
    spans = [(0, half), (half, width), (half + width, half)]
    copies = [pltpu.make_async_copy(index_ref, indices, sems.at[0])]
    for e in range(3):
        start, (to, size) = pl.multiple_of(starts[e], half), spans[e]
        copies.append(
            pltpu.make_async_copy(
                tokens_ref.at[:, :, pl.ds(start, size)],
                held.at[:, :, to : to + size],
                sems.at[1 + e],
            )
        )
    copies.append(pltpu.make_async_copy(down_ref.at[:, :, :half], lower_ref, sems.at[4]))
    copies.append(pltpu.make_async_copy(down_ref.at[:, :, half:], upper_ref, sems.at[5]))
    for copy in copies:
        copy.start()
    copies[0].wait()
    wide, place, label = read_index(indices, owned)
    rows = wide.shape[0]
    line, column = iota((rows, rows), 0), iota((rows, rows), 1)
    hit = line == wide
    label = jnp.broadcast_to(label, (rows, rows))
    labels = [
        jnp.sum(jnp.where(hit & (place == p), label, 0.0), axis=1, keepdims=True)
        for p in (0.0, 1.0)
    ]
    labels = jnp.where(column < 64, labels[0], labels[1]).astype(BF16)
    out_ref[:, :, 2 * width :] = labels.reshape(rows // 2, 2, 128)
    select = jnp.where(hit & (place == parity.astype(F32)), 1.0, 0.0).astype(BF16)
    for copy in copies[1:4]:
        copy.wait()
    tokens = held[...].reshape(rows, 2 * width)
    packed = jnp.dot(select, tokens, preferred_element_type=F32).astype(BF16)
    out_ref[:, :, : 2 * width] = packed.reshape(rows // 2, 2, 2 * width)
    for copy in copies[4:]:
        copy.wait()


def shrink_kernel(received_ref, before_ref, own_ref, after_ref, partial_ref, label_ref):
    shards, groups, width = received_ref.shape
    width = (width - 128) // 2
    lines = shards * groups
    parity = lax.axis_index("tensor") % 2
    product, at = None, 0
    for weight_ref in (before_ref, own_ref, after_ref):
        size = weight_ref.shape[2]
        rows = received_ref[:, :, at : at + size].reshape(lines, size)
        mine = lax.dot_general(
            rows,
            weight_ref[...].reshape(256, size),
            (((1,), (1,)), ((), ())),
            preferred_element_type=F32,
        )
        product = mine if at == 0 else product + mine
        at += size
    label = received_ref[:, :, 2 * width :].reshape(lines, 128).astype(F32)
    turned = pltpu.roll(label, 64, 1)
    upper = iota((lines, 128), 1) // 64
    here = jnp.where(upper == parity, label, turned)
    total = jnp.where(here == upper.astype(F32) + 1.0, product[:, :128], 0.0)
    total = total + jnp.where(here == upper.astype(F32) + 3.0, product[:, 128:], 0.0)
    total = total + pltpu.roll(total, 64, 1)
    half = lines // 2
    packed = jnp.where(upper[:half] == 0, total[:half], total[half:]).astype(BF16)
    for peer in range(partial_ref.shape[0]):
        partial_ref[peer] = packed
    low = jnp.where(upper == 0, label, turned)
    high = jnp.where(upper == 0, turned, label)
    label_ref[...] = spread(low, high).astype(BF16)


def expand_kernel(partial_ref, label_ref, up_ref, out_ref):
    sums = []
    for p in range(2):
        total = partial_ref[p].astype(F32)
        for peer in range(p + 2, partial_ref.shape[0], 2):
            total = total + partial_ref[peer].astype(F32)
        sums.append(total)
    total = spread(*sums)
    turned = pltpu.roll(total, 64, 1)
    upper = iota(total.shape, 1) // 64
    lines = total.shape[0]
    for e in range(2):
        row = jnp.where(upper == e, total, turned)
        label = label_ref[e * lines : (e + 1) * lines].astype(F32)
        left = jnp.where(label == upper.astype(F32) + 1.0, row, 0.0)
        right = jnp.where(label == upper.astype(F32) + 3.0, row, 0.0)
        wide = jnp.concatenate([left, right], axis=1).astype(BF16)
        out_ref[e * lines : (e + 1) * lines] = jnp.dot(
            wide, up_ref[...], preferred_element_type=F32
        )


def place_kernel(owned, index_ref, out_ref):
    wide, place, _ = read_index(index_ref, owned)
    rows = wide.shape[0]
    key = wide[:1]
    target = (key >> 1) * 4 + place.astype(I32) * 2 + (key & 1)
    line, column = iota((rows, rows), 0), iota((rows, rows), 1)
    target = jnp.broadcast_to(target, (rows, rows))
    target = jnp.sum(jnp.where(line == column, target, 0).astype(F32), axis=1, keepdims=True)
    out_ref[...] = jnp.where(iota(out_ref.shape, 1).astype(F32) == target, 1.0, 0.0).astype(BF16)


def add_kernel(place_ref, arrived_ref, base_ref, out_ref):
    arrived = arrived_ref[...]
    high = arrived.astype(BF16)
    low = (arrived - high.astype(F32)).astype(BF16)
    place = place_ref[...]
    terms = jnp.dot(place, high, preferred_element_type=F32) + jnp.dot(
        place, low, preferred_element_type=F32
    )
    out_ref[...] = (base_ref[...] + terms).astype(BF16)


def call(kernel, shapes, ins, scratch=(), in_hbm=(), out_hbm=(), vmem=40):
    nbytes = sum(v.size * v.dtype.itemsize for v in ins)

    def spec(hbm):
        return pl.BlockSpec(memory_space=pltpu.HBM if hbm else pltpu.VMEM)

    return pl.pallas_call(
        kernel,
        out_shape=shapes,
        in_specs=[spec(i in in_hbm) for i in range(len(ins))],
        out_specs=[spec(i in out_hbm) for i in range(len(shapes))],
        scratch_shapes=scratch,
        compiler_params=pltpu.CompilerParams(vmem_limit_bytes=vmem * MIB),
        cost_estimate=pl.CostEstimate(flops=0, bytes_accessed=nbytes, transcendentals=0),
    )(*ins)


def on_device(tokens, value_matrix, down, up, index):
    groups, rows_local, features = tokens.shape
    owners = lax.axis_size("dp")
    planes = lax.axis_size("tensor")
    owned, width, rank = down.shape
    columns = up.shape[2]
    rows = groups * rows_local
    shape = jax.ShapeDtypeStruct

    down_own = down.transpose(0, 2, 1)
    piece = shape((owned, rank, width // 2), BF16)
    packed, lower, upper = call(
        functools.partial(pack_kernel, owned, planes),
        [shape((owners, groups, 2 * width + 128), BF16), piece, piece],
        (index, tokens, down_own),
        [
            pltpu.VMEM((groups, rows_local, 2 * width), BF16),
            pltpu.VMEM(index.shape, I32),
            pltpu.SemaphoreType.DMA((6,)),
        ],
        in_hbm=(0, 1, 2),
        out_hbm=(1, 2),
        vmem=62,
    )
    received = lax.all_to_all(packed, "dp", split_axis=0, concat_axis=0, tiled=True)
    before = lax.ppermute(upper, "tensor", [(i, (i + 1) % planes) for i in range(planes)])
    after = lax.ppermute(lower, "tensor", [(i, (i - 1) % planes) for i in range(planes)])

    base = jnp.dot(tokens.reshape(rows, features), value_matrix, preferred_element_type=F32)
    (place,) = call(
        functools.partial(place_kernel, owned), [shape((rows, owners * 4), BF16)], (index,)
    )
    partial, label = call(
        shrink_kernel,
        [shape((planes, owners, 128), BF16), shape((owners * 4, 128), BF16)],
        (received, before, down_own, after),
    )
    partials = lax.all_to_all(partial, "tensor", split_axis=0, concat_axis=0, tiled=True)
    (terms,) = call(
        expand_kernel,
        [shape((owners * 4, columns), F32)],
        (partials, label, up.reshape(owned * rank, columns)),
    )
    arrived = lax.all_to_all(
        terms.reshape(owners, 4, columns), "dp", split_axis=0, concat_axis=0, tiled=True
    ).reshape(owners * 4, columns)
    (out,) = call(add_kernel, [shape((rows, columns), BF16)], (place, arrived, base))
    return out.reshape(groups, rows_local, columns)


def solution(mesh):
    in_specs = (
        P(None, "dp", None),
        P(None, "tensor"),
        P("dp", "tensor", None),
        P("dp", None, "tensor"),
        P(None, "dp"),
    )
    out_specs = P(None, "dp", "tensor")
    return jax.shard_map(
        on_device, mesh=mesh, in_specs=in_specs, out_specs=out_specs, check_vma=False
    )
```

```python
import functools

import jax
import jax.numpy as jnp
from jax import lax
from jax.experimental import pallas as pl
from jax.experimental.pallas import tpu as pltpu
from jax.sharding import PartitionSpec as P

BF16, F32, I32 = jnp.bfloat16, jnp.float32, jnp.int32
MIB = 1024 * 1024


def iota(shape, dim):
    return lax.broadcasted_iota(I32, shape, dim)


def read_index(index_ref, owned):
    along = jnp.concatenate([index_ref[0:1, :], index_ref[1:2, :]], axis=1)
    rows = along.shape[1]
    shift = owned.bit_length() - 1
    assert owned == 1 << shift
    key = (along >> shift) * 2 + jnp.where(iota((1, rows), 1) >= rows // 2, 1, 0)
    wide = jnp.broadcast_to(key, (rows, rows))
    line, column = iota((rows, rows), 0), iota((rows, rows), 1)
    same = jnp.sum(jnp.where(line == column, wide, 0).astype(F32), axis=1, keepdims=True)
    earlier = (wide.astype(F32) == same) & (line < column)
    place = jnp.sum(jnp.where(earlier, 1.0, 0.0), axis=0, keepdims=True)
    return wide, place, ((along & (owned - 1)) + 1).astype(F32)


def spread(first, second):
    first, second = (v.reshape(v.shape[0] // 8, 8, 128) for v in (first, second))
    pair = iota(first.shape, 1) // 2

    def turn(total, by):
        return pltpu.roll(total, by, 1)

    def pick(*pieces):
        out = pieces[0]
        for d in range(1, 4):
            out = jnp.where(pair == d, pieces[d], out)
        return out

    even = pick(first, turn(second, 2), turn(first, 2), turn(second, 4))
    odd = pick(turn(first, 4), turn(second, 6), turn(first, 6), second)
    return jnp.stack([even, odd], axis=1).reshape(first.shape[0] * 16, 128)


def pack_kernel(owned, planes, index_ref, tokens_ref, out_ref, held, indices, sems):
    features = tokens_ref.shape[2]
    width = features // planes
    half = width // 2
    plane = lax.axis_index("tensor")
    parity = plane % 2
    starts = [(plane * width + features - half) % features, plane * width]
    starts.append((plane * width + width) % features)
    spans = [(0, half), (half, width), (half + width, half)]
    copies = [pltpu.make_async_copy(index_ref, indices, sems.at[0])]
    for e in range(3):
        start, (to, size) = pl.multiple_of(starts[e], half), spans[e]
        copies.append(
            pltpu.make_async_copy(
                tokens_ref.at[:, :, pl.ds(start, size)],
                held.at[:, :, to : to + size],
                sems.at[1 + e],
            )
        )
    for copy in copies:
        copy.start()
    copies[0].wait()
    wide, place, label = read_index(indices, owned)
    rows = wide.shape[0]
    line, column = iota((rows, rows), 0), iota((rows, rows), 1)
    hit = line == wide
    label = jnp.broadcast_to(label, (rows, rows))
    labels = [
        jnp.sum(jnp.where(hit & (place == p), label, 0.0), axis=1, keepdims=True)
        for p in (0.0, 1.0)
    ]
    labels = jnp.where(column < 64, labels[0], labels[1]).astype(BF16)
    out_ref[:, :, 2 * width :] = labels.reshape(rows // 2, 2, 128)
    select = jnp.where(hit & (place == parity.astype(F32)), 1.0, 0.0).astype(BF16)
    for copy in copies[1:]:
        copy.wait()
    tokens = held[...].reshape(rows, 2 * width)
    packed = jnp.dot(select, tokens, preferred_element_type=F32).astype(BF16)
    out_ref[:, :, : 2 * width] = packed.reshape(rows // 2, 2, 2 * width)


def shrink_kernel(received_ref, before_ref, own_ref, after_ref, partial_ref, label_ref):
    shards, groups, width = received_ref.shape
    width = (width - 128) // 2
    lines = shards * groups
    parity = lax.axis_index("tensor") % 2
    product, at = None, 0
    for weight_ref in (before_ref, own_ref, after_ref):
        size = weight_ref.shape[2]
        rows = received_ref[:, :, at : at + size].reshape(lines, size)
        mine = lax.dot_general(
            rows,
            weight_ref[...].reshape(256, size),
            (((1,), (1,)), ((), ())),
            preferred_element_type=F32,
        )
        product = mine if at == 0 else product + mine
        at += size
    label = received_ref[:, :, 2 * width :].reshape(lines, 128).astype(F32)
    turned = pltpu.roll(label, 64, 1)
    upper = iota((lines, 128), 1) // 64
    here = jnp.where(upper == parity, label, turned)
    total = jnp.where(here == upper.astype(F32) + 1.0, product[:, :128], 0.0)
    total = total + jnp.where(here == upper.astype(F32) + 3.0, product[:, 128:], 0.0)
    total = total + pltpu.roll(total, 64, 1)
    half = lines // 2
    packed = jnp.where(upper[:half] == 0, total[:half], total[half:]).astype(BF16)
    for peer in range(partial_ref.shape[0]):
        partial_ref[peer] = packed
    low = jnp.where(upper == 0, label, turned)
    high = jnp.where(upper == 0, turned, label)
    label_ref[...] = spread(low, high).astype(BF16)


def expand_kernel(partial_ref, label_ref, up_ref, out_ref):
    sums = []
    for p in range(2):
        total = partial_ref[p].astype(F32)
        for peer in range(p + 2, partial_ref.shape[0], 2):
            total = total + partial_ref[peer].astype(F32)
        sums.append(total)
    total = spread(*sums)
    turned = pltpu.roll(total, 64, 1)
    upper = iota(total.shape, 1) // 64
    lines = total.shape[0]
    for e in range(2):
        row = jnp.where(upper == e, total, turned)
        label = label_ref[e * lines : (e + 1) * lines].astype(F32)
        left = jnp.where(label == upper.astype(F32) + 1.0, row, 0.0)
        right = jnp.where(label == upper.astype(F32) + 3.0, row, 0.0)
        wide = jnp.concatenate([left, right], axis=1).astype(BF16)
        out_ref[e * lines : (e + 1) * lines] = jnp.dot(
            wide, up_ref[...], preferred_element_type=F32
        )


def place_kernel(owned, index_ref, out_ref):
    wide, place, _ = read_index(index_ref, owned)
    rows = wide.shape[0]
    key = wide[:1]
    target = (key >> 1) * 4 + place.astype(I32) * 2 + (key & 1)
    line, column = iota((rows, rows), 0), iota((rows, rows), 1)
    target = jnp.broadcast_to(target, (rows, rows))
    target = jnp.sum(jnp.where(line == column, target, 0).astype(F32), axis=1, keepdims=True)
    out_ref[...] = jnp.where(iota(out_ref.shape, 1).astype(F32) == target, 1.0, 0.0).astype(BF16)


def add_kernel(place_ref, arrived_ref, base_ref, out_ref):
    arrived = arrived_ref[...]
    high = arrived.astype(BF16)
    low = (arrived - high.astype(F32)).astype(BF16)
    place = place_ref[...]
    terms = jnp.dot(place, high, preferred_element_type=F32) + jnp.dot(
        place, low, preferred_element_type=F32
    )
    out_ref[...] = (base_ref[...] + terms).astype(BF16)


def call(kernel, shapes, ins, scratch=(), in_hbm=(), vmem=40):
    nbytes = sum(v.size * v.dtype.itemsize for v in ins)

    def spec(hbm):
        return pl.BlockSpec(memory_space=pltpu.HBM if hbm else pltpu.VMEM)

    return pl.pallas_call(
        kernel,
        out_shape=shapes,
        in_specs=[spec(i in in_hbm) for i in range(len(ins))],
        out_specs=[spec(False) for _ in shapes],
        scratch_shapes=scratch,
        compiler_params=pltpu.CompilerParams(vmem_limit_bytes=vmem * MIB),
        cost_estimate=pl.CostEstimate(flops=0, bytes_accessed=nbytes, transcendentals=0),
    )(*ins)


def on_device(tokens, value_matrix, down, up, index):
    groups, rows_local, features = tokens.shape
    owners = lax.axis_size("dp")
    planes = lax.axis_size("tensor")
    owned, width, rank = down.shape
    columns = up.shape[2]
    rows = groups * rows_local
    shape = jax.ShapeDtypeStruct

    (packed,) = call(
        functools.partial(pack_kernel, owned, planes),
        [shape((owners, groups, 2 * width + 128), BF16)],
        (index, tokens),
        [
            pltpu.VMEM((groups, rows_local, 2 * width), BF16),
            pltpu.VMEM(index.shape, I32),
            pltpu.SemaphoreType.DMA((4,)),
        ],
        in_hbm=(0, 1),
        vmem=62,
    )
    received = lax.all_to_all(packed, "dp", split_axis=0, concat_axis=0, tiled=True)

    down_own = down.transpose(0, 2, 1)
    later, _ = lax.optimization_barrier((down_own, packed))
    upper, lower = later[:, :, width // 2 :], later[:, :, : width // 2]
    before = lax.ppermute(upper, "tensor", [(i, (i + 1) % planes) for i in range(planes)])
    after = lax.ppermute(lower, "tensor", [(i, (i - 1) % planes) for i in range(planes)])

    base = jnp.dot(tokens.reshape(rows, features), value_matrix, preferred_element_type=F32)
    (place,) = call(
        functools.partial(place_kernel, owned), [shape((rows, owners * 4), BF16)], (index,)
    )
    partial, label = call(
        shrink_kernel,
        [shape((planes, owners, 128), BF16), shape((owners * 4, 128), BF16)],
        (received, before, down_own, after),
    )
    partials = lax.all_to_all(partial, "tensor", split_axis=0, concat_axis=0, tiled=True)
    (terms,) = call(
        expand_kernel,
        [shape((owners * 4, columns), F32)],
        (partials, label, up.reshape(owned * rank, columns)),
    )
    arrived = lax.all_to_all(
        terms.reshape(owners, 4, columns), "dp", split_axis=0, concat_axis=0, tiled=True
    ).reshape(owners * 4, columns)
    (out,) = call(add_kernel, [shape((rows, columns), BF16)], (place, arrived, base))
    return out.reshape(groups, rows_local, columns)


def solution(mesh):
    in_specs = (
        P(None, "dp", None),
        P(None, "tensor"),
        P("dp", "tensor", None),
        P("dp", None, "tensor"),
        P(None, "dp"),
    )
    out_specs = P(None, "dp", "tensor")
    return jax.shard_map(
        on_device, mesh=mesh, in_specs=in_specs, out_specs=out_specs, check_vma=False
    )
```

```python
import functools

import jax
import jax.numpy as jnp
from jax import lax
from jax.experimental import pallas as pl
from jax.experimental.pallas import tpu as pltpu
from jax.sharding import PartitionSpec as P

BF16, F32, I32 = jnp.bfloat16, jnp.float32, jnp.int32
MIB = 1024 * 1024


def iota(shape, dim):
    return lax.broadcasted_iota(I32, shape, dim)


def read_index(index_ref, owned):
    along = jnp.concatenate([index_ref[0:1, :], index_ref[1:2, :]], axis=1)
    rows = along.shape[1]
    shift = owned.bit_length() - 1
    assert owned == 1 << shift
    key = (along >> shift) * 2 + jnp.where(iota((1, rows), 1) >= rows // 2, 1, 0)
    wide = jnp.broadcast_to(key, (rows, rows))
    line, column = iota((rows, rows), 0), iota((rows, rows), 1)
    same = jnp.sum(jnp.where(line == column, wide, 0).astype(F32), axis=1, keepdims=True)
    earlier = (wide.astype(F32) == same) & (line < column)
    place = jnp.sum(jnp.where(earlier, 1.0, 0.0), axis=0, keepdims=True)
    return wide, place, ((along & (owned - 1)) + 1).astype(F32)


def over_lanes(values):
    share = jnp.full((128, 128), 1.0 / 32.0, BF16)
    return jnp.dot(values.astype(BF16), share, preferred_element_type=F32)


def pack_kernel(owned, planes, index_ref, tokens_ref, out_ref, held, indices, sems):
    features = tokens_ref.shape[2]
    width = features // planes
    half = width // 2
    plane = lax.axis_index("tensor")
    parity = plane % 2
    starts = [(plane * width + features - half) % features, plane * width]
    starts.append((plane * width + width) % features)
    spans = [(0, half), (half, width), (half + width, half)]
    copies = [pltpu.make_async_copy(index_ref, indices, sems.at[0])]
    for e in range(3):
        start, (to, size) = pl.multiple_of(starts[e], half), spans[e]
        copies.append(
            pltpu.make_async_copy(
                tokens_ref.at[:, :, pl.ds(start, size)],
                held.at[:, :, to : to + size],
                sems.at[1 + e],
            )
        )
    for copy in copies:
        copy.start()
    copies[0].wait()
    wide, place, label = read_index(indices, owned)
    rows = wide.shape[0]
    line, column = iota((rows, rows), 0), iota((rows, rows), 1)
    hit = line == wide
    label = jnp.broadcast_to(label, (rows, rows))
    labels = None
    for field in range(4):
        core, p = field // 2, float(field % 2)
        chip_hit = wide == (line & -4) + 2 * core + (line & 1)
        found = jnp.where(chip_hit & (place == p), label, 0.0)
        found = jnp.sum(found, axis=1, keepdims=True)
        labels = found if field == 0 else jnp.where(column // 32 == field, found, labels)
    labels = jnp.broadcast_to(labels, (rows, 128)).astype(BF16)
    out_ref[:, :, 2 * width :] = labels.reshape(rows // 2, 2, 128)
    select = jnp.where(hit & (place == parity.astype(F32)), 1.0, 0.0).astype(BF16)
    for copy in copies[1:]:
        copy.wait()
    tokens = held[...].reshape(rows, 2 * width)
    packed = jnp.dot(select, tokens, preferred_element_type=F32).astype(BF16)
    out_ref[:, :, : 2 * width] = packed.reshape(rows // 2, 2, 2 * width)


def shrink_kernel(received_ref, before_ref, own_ref, after_ref, partial_ref):
    shards, groups, width = received_ref.shape
    width = (width - 128) // 2
    lines = shards * groups
    parity = lax.axis_index("tensor") % 2
    core = lax.axis_index("dp") % 2
    product, at = None, 0
    for weight_ref in (before_ref, own_ref, after_ref):
        size = weight_ref.shape[2]
        rows = received_ref[:, :, at : at + size].reshape(lines, size)
        mine = lax.dot_general(
            rows,
            weight_ref[...].reshape(256, size),
            (((1,), (1,)), ((), ())),
            preferred_element_type=F32,
        )
        product = mine if at == 0 else product + mine
        at += size
    label = received_ref[:, :, 2 * width :].reshape(lines, 128)
    field = iota((lines, 128), 1) // 32
    here = over_lanes(jnp.where(field == core * 2 + parity, label.astype(F32), 0.0))
    upper = (iota((lines, 128), 1) // 64).astype(F32)
    total = jnp.where(here == upper + 1.0, product[:, :128], 0.0)
    total = total + jnp.where(here == upper + 3.0, product[:, 128:], 0.0)
    total = total + pltpu.roll(total, 64, 1)
    half = lines // 2
    packed = jnp.where(upper[:half] == 0.0, total[:half], total[half:])
    chips = packed.reshape(half // 8, 8, 128)
    for c in range(2):
        by_pair = chips.reshape(half // 16, 2, 8, 128)
        left, right = by_pair[:, 0], by_pair[:, 1]
        place = iota(left.shape, 1) // 2
        turn = pltpu.roll
        if c == 0:
            pieces = [left, turn(left, 6, 1), turn(right, 4, 1), turn(right, 2, 1)]
        else:
            pieces = [turn(left, 6, 1), turn(left, 4, 1), turn(right, 2, 1), right]
        out = pieces[0]
        for d in range(1, 4):
            out = jnp.where(place == d, pieces[d], out)
        out = out.reshape(half // 2, 128).astype(BF16)
        planes = partial_ref.shape[0] // 2
        for peer in range(planes):
            partial_ref[c * planes + peer] = out


def label_kernel(received_ref, out_ref):
    shards, groups, width = received_ref.shape
    label = received_ref[:, :, width - 128 :].reshape(shards * groups, 128)
    core = lax.axis_index("dp") % 2
    lines = out_ref.shape[0]
    line = iota((lines, shards * groups), 0)
    source = (line // 8 * 2 + core) * 2 + line % 2
    take = jnp.where(iota((lines, shards * groups), 1) == source, 1.0, 0.0).astype(BF16)
    label = jnp.dot(take, label, preferred_element_type=F32)
    line = iota((lines, 128), 0)
    label = over_lanes(jnp.where(iota((lines, 128), 1) // 32 == line // 2 % 4, label, 0.0))
    other = (label > 0.0) & (line // 4 % 2 != core)
    out_ref[...] = jnp.where(other, label + 4.0, label).astype(BF16)


def expand_kernel(partial_ref, label_ref, up_own_ref, up_other_ref, out_ref):
    planes, half, _ = partial_ref.shape
    planes //= 2
    sums = []
    for core in range(2):
        for p in range(2):
            total = partial_ref[core * planes + p].astype(F32)
            for peer in range(p + 2, planes, 2):
                total = total + partial_ref[core * planes + peer].astype(F32)
            sums.append(total.reshape(half // 8, 8, 128))
    place = iota(sums[0].shape, 1) // 2
    by_chip = []
    for chip in range(4):
        out = None
        for field in range(4):
            by = 2 * (field - chip) % 8
            piece = pltpu.roll(sums[field], by, 1) if by else sums[field]
            out = piece if field == 0 else jnp.where(place == field, piece, out)
        by_chip.append(out)
    total = jnp.stack(by_chip, axis=1).reshape(half * 4, 128)
    turned = pltpu.roll(total, 64, 1)
    upper = iota(total.shape, 1) // 64
    lines = total.shape[0]
    for e in range(2):
        row = jnp.where(upper == e, total, turned)
        label = label_ref[e * lines : (e + 1) * lines].astype(F32)
        terms = None
        for up_ref, add in ((up_own_ref, 1.0), (up_other_ref, 5.0)):
            first = upper.astype(F32) + add
            left = jnp.where(label == first, row, 0.0)
            right = jnp.where(label == first + 2.0, row, 0.0)
            wide = jnp.concatenate([left, right], axis=1).astype(BF16)
            mine = jnp.dot(wide, up_ref[...], preferred_element_type=F32)
            terms = mine if terms is None else terms + mine
        out_ref[e * lines : (e + 1) * lines] = terms


def place_kernel(owned, index_ref, out_ref):
    wide, place, _ = read_index(index_ref, owned)
    rows = wide.shape[0]
    key = wide[:1]
    target = (key >> 1) * 4 + place.astype(I32) * 2 + (key & 1)
    line, column = iota((rows, rows), 0), iota((rows, rows), 1)
    target = jnp.broadcast_to(target, (rows, rows))
    target = jnp.sum(jnp.where(line == column, target, 0).astype(F32), axis=1, keepdims=True)
    out_ref[...] = jnp.where(iota(out_ref.shape, 1).astype(F32) == target, 1.0, 0.0).astype(BF16)


def add_kernel(place_ref, arrived_ref, base_ref, out_ref):
    arrived = arrived_ref[...]
    high = arrived.astype(BF16)
    low = (arrived - high.astype(F32)).astype(BF16)
    place = place_ref[...]
    terms = jnp.dot(place, high, preferred_element_type=F32) + jnp.dot(
        place, low, preferred_element_type=F32
    )
    out_ref[...] = (base_ref[...] + terms).astype(BF16)


def call(kernel, shapes, ins, scratch=(), in_hbm=(), vmem=40):
    nbytes = sum(v.size * v.dtype.itemsize for v in ins)

    def spec(hbm):
        return pl.BlockSpec(memory_space=pltpu.HBM if hbm else pltpu.VMEM)

    return pl.pallas_call(
        kernel,
        out_shape=shapes,
        in_specs=[spec(i in in_hbm) for i in range(len(ins))],
        out_specs=[spec(False) for _ in shapes],
        scratch_shapes=scratch,
        compiler_params=pltpu.CompilerParams(vmem_limit_bytes=vmem * MIB),
        cost_estimate=pl.CostEstimate(flops=0, bytes_accessed=nbytes, transcendentals=0),
    )(*ins)


def on_device(tokens, value_matrix, down, up, index):
    groups, rows_local, features = tokens.shape
    owners = lax.axis_size("dp")
    planes = lax.axis_size("tensor")
    owned, width, rank = down.shape
    columns = up.shape[2]
    rows = groups * rows_local
    shape = jax.ShapeDtypeStruct

    (packed,) = call(
        functools.partial(pack_kernel, owned, planes),
        [shape((owners, groups, 2 * width + 128), BF16)],
        (index, tokens),
        [
            pltpu.VMEM((groups, rows_local, 2 * width), BF16),
            pltpu.VMEM(index.shape, I32),
            pltpu.SemaphoreType.DMA((4,)),
        ],
        in_hbm=(0, 1),
        vmem=62,
    )
    received = lax.all_to_all(packed, "dp", split_axis=0, concat_axis=0, tiled=True)

    down_own, up_own = down.transpose(0, 2, 1), up.reshape(owned * rank, columns)
    later, up_later, _ = lax.optimization_barrier((down_own, up_own, packed))
    upper, lower = later[:, :, width // 2 :], later[:, :, : width // 2]
    before = lax.ppermute(upper, "tensor", [(i, (i + 1) % planes) for i in range(planes)])
    after = lax.ppermute(lower, "tensor", [(i, (i - 1) % planes) for i in range(planes)])
    up_other = lax.ppermute(up_later, "dp", [(i, i ^ 1) for i in range(owners)])

    base = jnp.dot(tokens.reshape(rows, features), value_matrix, preferred_element_type=F32)
    (place,) = call(
        functools.partial(place_kernel, owned), [shape((rows, owners * 4), BF16)], (index,)
    )
    (partial,) = call(
        shrink_kernel,
        [shape((2 * planes, owners // 2, 128), BF16)],
        (received, before, down_own, after),
    )
    chips = [list(range(i, i + 2 * planes)) for i in range(0, owners * planes, 2 * planes)]
    partials = lax.all_to_all(
        partial, ("dp", "tensor"), split_axis=0, concat_axis=0, tiled=True, axis_index_groups=chips
    )
    (label,) = call(label_kernel, [shape((owners * 4, 128), BF16)], (received,))
    (terms,) = call(
        expand_kernel,
        [shape((owners * 4, columns), F32)],
        (partials, label, up_own, up_other),
    )
    arrived = lax.all_to_all(
        terms.reshape(owners // 2, 8, columns),
        "dp",
        split_axis=0,
        concat_axis=0,
        tiled=True,
        axis_index_groups=[list(range(core, owners, 2)) for core in range(2)],
    ).reshape(owners * 4, columns)
    (out,) = call(add_kernel, [shape((rows, columns), BF16)], (place, arrived, base))
    return out.reshape(groups, rows_local, columns)


def solution(mesh):
    in_specs = (
        P(None, "dp", None),
        P(None, "tensor"),
        P("dp", "tensor", None),
        P("dp", None, "tensor"),
        P(None, "dp"),
    )
    out_specs = P(None, "dp", "tensor")
    return jax.shard_map(
        on_device, mesh=mesh, in_specs=in_specs, out_specs=out_specs, check_vma=False
    )
```

```python
import functools

import jax
import jax.numpy as jnp
from jax import lax
from jax.experimental import pallas as pl
from jax.experimental.pallas import tpu as pltpu
from jax.sharding import PartitionSpec as P

BF16, F32, I32 = jnp.bfloat16, jnp.float32, jnp.int32
MIB = 1024 * 1024


def iota(shape, dim):
    return lax.broadcasted_iota(I32, shape, dim)


def read_index(index_ref, owned):
    along = jnp.concatenate([index_ref[0:1, :], index_ref[1:2, :]], axis=1)
    rows = along.shape[1]
    shift = owned.bit_length() - 1
    assert owned == 1 << shift
    key = (along >> shift) * 2 + jnp.where(iota((1, rows), 1) >= rows // 2, 1, 0)
    wide = jnp.broadcast_to(key, (rows, rows))
    line, column = iota((rows, rows), 0), iota((rows, rows), 1)
    same = jnp.sum(jnp.where(line == column, wide, 0).astype(F32), axis=1, keepdims=True)
    earlier = (wide.astype(F32) == same) & (line < column)
    place = jnp.sum(jnp.where(earlier, 1.0, 0.0), axis=0, keepdims=True)
    return wide, place, ((along & (owned - 1)) + 1).astype(F32)


def over_lanes(values):
    share = jnp.full((128, 128), 1.0 / 32.0, BF16)
    return jnp.dot(values.astype(BF16), share, preferred_element_type=F32)


def pack_kernel(owned, planes, index_ref, tokens_ref, out_ref, held, indices, sems):
    features = tokens_ref.shape[2]
    width = features // planes
    half = width // 2
    plane = lax.axis_index("tensor")
    parity = plane % 2
    starts = [(plane * width + features - half) % features, plane * width]
    starts.append((plane * width + width) % features)
    spans = [(0, half), (half, width), (half + width, half)]
    copies = [pltpu.make_async_copy(index_ref, indices, sems.at[0])]
    for e in range(3):
        start, (to, size) = pl.multiple_of(starts[e], half), spans[e]
        copies.append(
            pltpu.make_async_copy(
                tokens_ref.at[:, :, pl.ds(start, size)],
                held.at[:, :, to : to + size],
                sems.at[1 + e],
            )
        )
    for copy in copies:
        copy.start()
    copies[0].wait()
    wide, place, label = read_index(indices, owned)
    rows = wide.shape[0]
    line, column = iota((rows, rows), 0), iota((rows, rows), 1)
    hit = line == wide
    label = jnp.broadcast_to(label, (rows, rows))
    labels = None
    for field in range(4):
        core, p = field // 2, float(field % 2)
        chip_hit = wide == (line & -4) + 2 * core + (line & 1)
        found = jnp.where(chip_hit & (place == p), label, 0.0)
        found = jnp.sum(found, axis=1, keepdims=True)
        labels = found if field == 0 else jnp.where(column // 32 == field, found, labels)
    labels = jnp.broadcast_to(labels, (rows, 128)).astype(BF16)
    out_ref[:, :, 2 * width :] = labels.reshape(rows // 2, 2, 128)
    select = jnp.where(hit & (place == parity.astype(F32)), 1.0, 0.0).astype(BF16)
    for copy in copies[1:]:
        copy.wait()
    tokens = held[...].reshape(rows, 2 * width)
    packed = jnp.dot(select, tokens, preferred_element_type=F32).astype(BF16)
    out_ref[:, :, : 2 * width] = packed.reshape(rows // 2, 2, 2 * width)


def shrink_kernel(received_ref, before_ref, own_ref, after_ref, partial_ref):
    shards, groups, width = received_ref.shape
    width = (width - 128) // 2
    lines = shards * groups
    parity = lax.axis_index("tensor") % 2
    core = lax.axis_index("dp") % 2
    product, at = None, 0
    for weight_ref in (before_ref, own_ref, after_ref):
        size = weight_ref.shape[2]
        rows = received_ref[:, :, at : at + size].reshape(lines, size)
        mine = lax.dot_general(
            rows,
            weight_ref[...].reshape(256, size),
            (((1,), (1,)), ((), ())),
            preferred_element_type=F32,
        )
        product = mine if at == 0 else product + mine
        at += size
    label = received_ref[:, :, 2 * width :].reshape(lines, 128)
    field = iota((lines, 128), 1) // 32
    here = over_lanes(jnp.where(field == core * 2 + parity, label.astype(F32), 0.0))
    upper = (iota((lines, 128), 1) // 64).astype(F32)
    total = jnp.where(here == upper + 1.0, product[:, :128], 0.0)
    total = total + jnp.where(here == upper + 3.0, product[:, 128:], 0.0)
    total = total + pltpu.roll(total, 64, 1)
    half = lines // 2
    packed = jnp.where(upper[:half] == 0.0, total[:half], total[half:])
    chips = packed.reshape(half // 8, 8, 128)
    for c in range(2):
        by_pair = chips.reshape(half // 16, 2, 8, 128)
        left, right = by_pair[:, 0], by_pair[:, 1]
        place = iota(left.shape, 1) // 2
        turn = pltpu.roll
        if c == 0:
            pieces = [left, turn(left, 6, 1), turn(right, 4, 1), turn(right, 2, 1)]
        else:
            pieces = [turn(left, 6, 1), turn(left, 4, 1), turn(right, 2, 1), right]
        out = pieces[0]
        for d in range(1, 4):
            out = jnp.where(place == d, pieces[d], out)
        out = out.reshape(half // 2, 128).astype(BF16)
        planes = partial_ref.shape[0] // 2
        for peer in range(planes):
            partial_ref[c * planes + peer] = out


def label_kernel(received_ref, out_ref):
    shards, groups, width = received_ref.shape
    label = received_ref[:, :, width - 128 :].reshape(shards * groups, 128)
    core = lax.axis_index("dp") % 2
    lines = out_ref.shape[0]
    line = iota((lines, shards * groups), 0)
    source = (line // 8 * 2 + core) * 2 + line % 2
    take = jnp.where(iota((lines, shards * groups), 1) == source, 1.0, 0.0).astype(BF16)
    label = jnp.dot(take, label, preferred_element_type=F32)
    line = iota((lines, 128), 0)
    label = over_lanes(jnp.where(iota((lines, 128), 1) // 32 == line // 2 % 4, label, 0.0))
    other = (label > 0.0) & (line // 4 % 2 != core)
    out_ref[...] = jnp.where(other, label + 4.0, label).astype(BF16)


def expand_kernel(partial_ref, label_ref, up_own_ref, up_other_ref, out_ref):
    planes, half, _ = partial_ref.shape
    planes //= 2
    sums = []
    for core in range(2):
        for p in range(2):
            total = partial_ref[core * planes + p].astype(F32)
            for peer in range(p + 2, planes, 2):
                total = total + partial_ref[core * planes + peer].astype(F32)
            sums.append(total.reshape(half // 8, 8, 128))
    place = iota(sums[0].shape, 1) // 2
    by_chip = []
    for chip in range(4):
        out = None
        for field in range(4):
            by = 2 * (field - chip) % 8
            piece = pltpu.roll(sums[field], by, 1) if by else sums[field]
            out = piece if field == 0 else jnp.where(place == field, piece, out)
        by_chip.append(out)
    total = jnp.stack(by_chip, axis=1).reshape(half * 4, 128)
    turned = pltpu.roll(total, 64, 1)
    upper = iota(total.shape, 1) // 64
    lines = total.shape[0]
    for e in range(2):
        row = jnp.where(upper == e, total, turned)
        label = label_ref[e * lines : (e + 1) * lines].astype(F32)
        terms = None
        for up_ref, add in ((up_own_ref, 1.0), (up_other_ref, 5.0)):
            first = upper.astype(F32) + add
            left = jnp.where(label == first, row, 0.0)
            right = jnp.where(label == first + 2.0, row, 0.0)
            wide = jnp.concatenate([left, right], axis=1)
            high = wide.astype(BF16)
            for part in (high, (wide - high.astype(F32)).astype(BF16)):
                mine = jnp.dot(part, up_ref[...], preferred_element_type=F32)
                terms = mine if terms is None else terms + mine
        out_ref[e * lines : (e + 1) * lines] = terms.astype(BF16)


def place_kernel(owned, index_ref, out_ref):
    wide, place, _ = read_index(index_ref, owned)
    rows = wide.shape[0]
    key = wide[:1]
    target = (key >> 1) * 4 + place.astype(I32) * 2 + (key & 1)
    line, column = iota((rows, rows), 0), iota((rows, rows), 1)
    target = jnp.broadcast_to(target, (rows, rows))
    target = jnp.sum(jnp.where(line == column, target, 0).astype(F32), axis=1, keepdims=True)
    out_ref[...] = jnp.where(iota(out_ref.shape, 1).astype(F32) == target, 1.0, 0.0).astype(BF16)


def add_kernel(place_ref, arrived_ref, base_ref, out_ref):
    terms = jnp.dot(place_ref[...], arrived_ref[...], preferred_element_type=F32)
    out_ref[...] = (base_ref[...] + terms).astype(BF16)


def call(kernel, shapes, ins, scratch=(), in_hbm=(), vmem=40):
    nbytes = sum(v.size * v.dtype.itemsize for v in ins)

    def spec(hbm):
        return pl.BlockSpec(memory_space=pltpu.HBM if hbm else pltpu.VMEM)

    return pl.pallas_call(
        kernel,
        out_shape=shapes,
        in_specs=[spec(i in in_hbm) for i in range(len(ins))],
        out_specs=[spec(False) for _ in shapes],
        scratch_shapes=scratch,
        compiler_params=pltpu.CompilerParams(vmem_limit_bytes=vmem * MIB),
        cost_estimate=pl.CostEstimate(flops=0, bytes_accessed=nbytes, transcendentals=0),
    )(*ins)


def on_device(tokens, value_matrix, down, up, index):
    groups, rows_local, features = tokens.shape
    owners = lax.axis_size("dp")
    planes = lax.axis_size("tensor")
    owned, width, rank = down.shape
    columns = up.shape[2]
    rows = groups * rows_local
    shape = jax.ShapeDtypeStruct

    (packed,) = call(
        functools.partial(pack_kernel, owned, planes),
        [shape((owners, groups, 2 * width + 128), BF16)],
        (index, tokens),
        [
            pltpu.VMEM((groups, rows_local, 2 * width), BF16),
            pltpu.VMEM(index.shape, I32),
            pltpu.SemaphoreType.DMA((4,)),
        ],
        in_hbm=(0, 1),
        vmem=62,
    )
    received = lax.all_to_all(packed, "dp", split_axis=0, concat_axis=0, tiled=True)

    down_own, up_own = down.transpose(0, 2, 1), up.reshape(owned * rank, columns)
    later, up_later, _ = lax.optimization_barrier((down_own, up_own, packed))
    upper, lower = later[:, :, width // 2 :], later[:, :, : width // 2]
    before = lax.ppermute(upper, "tensor", [(i, (i + 1) % planes) for i in range(planes)])
    after = lax.ppermute(lower, "tensor", [(i, (i - 1) % planes) for i in range(planes)])
    up_other = lax.ppermute(up_later, "dp", [(i, i ^ 1) for i in range(owners)])

    base = jnp.dot(tokens.reshape(rows, features), value_matrix, preferred_element_type=F32)
    (place,) = call(
        functools.partial(place_kernel, owned), [shape((rows, owners * 4), BF16)], (index,)
    )
    (partial,) = call(
        shrink_kernel,
        [shape((2 * planes, owners // 2, 128), BF16)],
        (received, before, down_own, after),
    )
    chips = [list(range(i, i + 2 * planes)) for i in range(0, owners * planes, 2 * planes)]
    partials = lax.all_to_all(
        partial, ("dp", "tensor"), split_axis=0, concat_axis=0, tiled=True, axis_index_groups=chips
    )
    (label,) = call(label_kernel, [shape((owners * 4, 128), BF16)], (received,))
    (terms,) = call(
        expand_kernel,
        [shape((owners * 4, columns), BF16)],
        (partials, label, up_own, up_other),
    )
    arrived = lax.all_to_all(
        terms.reshape(owners // 2, 8, columns),
        "dp",
        split_axis=0,
        concat_axis=0,
        tiled=True,
        axis_index_groups=[list(range(core, owners, 2)) for core in range(2)],
    ).reshape(owners * 4, columns)
    (out,) = call(add_kernel, [shape((rows, columns), BF16)], (place, arrived, base))
    return out.reshape(groups, rows_local, columns)


def solution(mesh):
    in_specs = (
        P(None, "dp", None),
        P(None, "tensor"),
        P("dp", "tensor", None),
        P("dp", None, "tensor"),
        P(None, "dp"),
    )
    out_specs = P(None, "dp", "tensor")
    return jax.shard_map(
        on_device, mesh=mesh, in_specs=in_specs, out_specs=out_specs, check_vma=False
    )
```

```python
import functools

import jax
import jax.numpy as jnp
from jax import lax
from jax.experimental import pallas as pl
from jax.experimental.pallas import tpu as pltpu
from jax.sharding import PartitionSpec as P

BF16, F32, I32 = jnp.bfloat16, jnp.float32, jnp.int32
MIB = 1024 * 1024


def iota(shape, dim):
    return lax.broadcasted_iota(I32, shape, dim)


def read_index(index_ref, owned):
    along = jnp.concatenate([index_ref[0:1, :], index_ref[1:2, :]], axis=1)
    rows = along.shape[1]
    shift = owned.bit_length() - 1
    assert owned == 1 << shift
    key = (along >> shift) * 2 + jnp.where(iota((1, rows), 1) >= rows // 2, 1, 0)
    wide = jnp.broadcast_to(key, (rows, rows))
    line, column = iota((rows, rows), 0), iota((rows, rows), 1)
    same = jnp.sum(jnp.where(line == column, wide, 0).astype(F32), axis=1, keepdims=True)
    earlier = (wide.astype(F32) == same) & (line < column)
    place = jnp.sum(jnp.where(earlier, 1.0, 0.0), axis=0, keepdims=True)
    return wide, place, ((along & (owned - 1)) + 1).astype(F32)


def over_lanes(values):
    share = jnp.full((128, 128), 1.0 / 32.0, BF16)
    return jnp.dot(values.astype(BF16), share, preferred_element_type=F32)


def pack_kernel(owned, planes, index_ref, tokens_ref, out_ref, held, indices, sems):
    features = tokens_ref.shape[2]
    width = features // planes
    half = width // 2
    plane = lax.axis_index("tensor")
    parity = plane % 2
    starts = [(plane * width + features - half) % features, plane * width]
    starts.append((plane * width + width) % features)
    spans = [(0, half), (half, width), (half + width, half)]
    copies = [pltpu.make_async_copy(index_ref, indices, sems.at[0])]
    for e in range(3):
        start, (to, size) = pl.multiple_of(starts[e], half), spans[e]
        copies.append(
            pltpu.make_async_copy(
                tokens_ref.at[:, :, pl.ds(start, size)],
                held.at[:, :, to : to + size],
                sems.at[1 + e],
            )
        )
    for copy in copies:
        copy.start()
    copies[0].wait()
    wide, place, label = read_index(indices, owned)
    rows = wide.shape[0]
    line, column = iota((rows, rows), 0), iota((rows, rows), 1)
    hit = line == wide
    label = jnp.broadcast_to(label, (rows, rows))
    labels = None
    for field in range(4):
        core, p = field // 2, float(field % 2)
        chip_hit = wide == (line & -4) + 2 * core + (line & 1)
        found = jnp.where(chip_hit & (place == p), label, 0.0)
        found = jnp.sum(found, axis=1, keepdims=True)
        labels = found if field == 0 else jnp.where(column >> 5 == field, found, labels)
    labels = jnp.broadcast_to(labels, (rows, 128)).astype(BF16)
    out_ref[:, :, 2 * width :] = labels.reshape(rows // 2, 2, 128)
    select = jnp.where(hit & (place == parity.astype(F32)), 1.0, 0.0).astype(BF16)
    for copy in copies[1:]:
        copy.wait()
    tokens = held[...].reshape(rows, 2 * width)
    packed = jnp.dot(select, tokens, preferred_element_type=F32).astype(BF16)
    out_ref[:, :, : 2 * width] = packed.reshape(rows // 2, 2, 2 * width)


def shrink_kernel(received_ref, before_ref, own_ref, after_ref, partial_ref, label_ref):
    shards, groups, width = received_ref.shape
    width = (width - 128) // 2
    lines = shards * groups
    parity = lax.axis_index("tensor") % 2
    core = lax.axis_index("dp") % 2
    product, at = None, 0
    for weight_ref in (before_ref, own_ref, after_ref):
        size = weight_ref.shape[2]
        rows = received_ref[:, :, at : at + size].reshape(lines, size)
        mine = lax.dot_general(
            rows,
            weight_ref[...].reshape(256, size),
            (((1,), (1,)), ((), ())),
            preferred_element_type=F32,
        )
        product = mine if at == 0 else product + mine
        at += size
    label = received_ref[:, :, 2 * width :].reshape(lines, 128)
    field = iota((lines, 128), 1) >> 5
    here = over_lanes(jnp.where(field == core * 2 + parity, label.astype(F32), 0.0))
    upper = (iota((lines, 128), 1) // 64).astype(F32)
    total = jnp.where(here == upper + 1.0, product[:, :128], 0.0)
    total = total + jnp.where(here == upper + 3.0, product[:, 128:], 0.0)
    total = total + pltpu.roll(total, 64, 1)
    half = lines // 2
    packed = jnp.where(upper[:half] == 0.0, total[:half], total[half:])
    chips = packed.reshape(half // 8, 8, 128)
    for c in range(2):
        by_pair = chips.reshape(half // 16, 2, 8, 128)
        left, right = by_pair[:, 0], by_pair[:, 1]
        place = iota(left.shape, 1) // 2
        turn = pltpu.roll
        if c == 0:
            pieces = [left, turn(left, 6, 1), turn(right, 4, 1), turn(right, 2, 1)]
        else:
            pieces = [turn(left, 6, 1), turn(left, 4, 1), turn(right, 2, 1), right]
        out = pieces[0]
        for d in range(1, 4):
            out = jnp.where(place == d, pieces[d], out)
        out = out.reshape(half // 2, 128).astype(BF16)
        planes = partial_ref.shape[0] // 2
        for peer in range(planes):
            partial_ref[c * planes + peer] = out
    out_lines = label_ref.shape[0]
    line = iota((out_lines, lines), 0)
    source = ((line >> 3) * 2 + core) * 2 + (line & 1)
    take = jnp.where(iota((out_lines, lines), 1) == source, 1.0, 0.0).astype(BF16)
    label = jnp.dot(take, label, preferred_element_type=F32)
    line = iota((out_lines, 128), 0)
    label = over_lanes(jnp.where(iota((out_lines, 128), 1) >> 5 == (line >> 1) & 3, label, 0.0))
    other = (label > 0.0) & ((line >> 2) & 1 != core)
    label_ref[...] = jnp.where(other, label + 4.0, label).astype(BF16)


def expand_kernel(partial_ref, label_ref, up_own_ref, up_other_ref, out_ref):
    planes, half, _ = partial_ref.shape
    planes //= 2
    sums = []
    for core in range(2):
        for p in range(2):
            total = partial_ref[core * planes + p].astype(F32)
            for peer in range(p + 2, planes, 2):
                total = total + partial_ref[core * planes + peer].astype(F32)
            sums.append(total.reshape(half // 8, 8, 128))
    place = iota(sums[0].shape, 1) // 2
    by_chip = []
    for chip in range(4):
        out = None
        for field in range(4):
            by = 2 * (field - chip) % 8
            piece = pltpu.roll(sums[field], by, 1) if by else sums[field]
            out = piece if field == 0 else jnp.where(place == field, piece, out)
        by_chip.append(out)
    total = jnp.stack(by_chip, axis=1).reshape(half * 4, 128)
    turned = pltpu.roll(total, 64, 1)
    upper = iota(total.shape, 1) // 64
    lines = total.shape[0]
    for e in range(2):
        row = jnp.where(upper == e, total, turned)
        label = label_ref[e * lines : (e + 1) * lines].astype(F32)
        terms = None
        for up_ref, add in ((up_own_ref, 1.0), (up_other_ref, 5.0)):
            first = upper.astype(F32) + add
            left = jnp.where(label == first, row, 0.0)
            right = jnp.where(label == first + 2.0, row, 0.0)
            wide = jnp.concatenate([left, right], axis=1)
            high = wide.astype(BF16)
            for part in (high, (wide - high.astype(F32)).astype(BF16)):
                mine = jnp.dot(part, up_ref[...], preferred_element_type=F32)
                terms = mine if terms is None else terms + mine
        out_ref[e * lines : (e + 1) * lines] = terms.astype(BF16)


def place_kernel(owned, index_ref, out_ref):
    wide, place, _ = read_index(index_ref, owned)
    rows = wide.shape[0]
    key = wide[:1]
    target = (key >> 1) * 4 + place.astype(I32) * 2 + (key & 1)
    line, column = iota((rows, rows), 0), iota((rows, rows), 1)
    target = jnp.broadcast_to(target, (rows, rows))
    target = jnp.sum(jnp.where(line == column, target, 0).astype(F32), axis=1, keepdims=True)
    out_ref[...] = jnp.where(iota(out_ref.shape, 1).astype(F32) == target, 1.0, 0.0).astype(BF16)


def add_kernel(place_ref, arrived_ref, base_ref, out_ref):
    terms = jnp.dot(place_ref[...], arrived_ref[...], preferred_element_type=F32)
    out_ref[...] = (base_ref[...] + terms).astype(BF16)


def call(kernel, shapes, ins, scratch=(), in_hbm=(), vmem=40):
    nbytes = sum(v.size * v.dtype.itemsize for v in ins)

    def spec(hbm):
        return pl.BlockSpec(memory_space=pltpu.HBM if hbm else pltpu.VMEM)

    return pl.pallas_call(
        kernel,
        out_shape=shapes,
        in_specs=[spec(i in in_hbm) for i in range(len(ins))],
        out_specs=[spec(False) for _ in shapes],
        scratch_shapes=scratch,
        compiler_params=pltpu.CompilerParams(vmem_limit_bytes=vmem * MIB),
        cost_estimate=pl.CostEstimate(flops=0, bytes_accessed=nbytes, transcendentals=0),
    )(*ins)


def on_device(tokens, value_matrix, down, up, index):
    groups, rows_local, features = tokens.shape
    owners = lax.axis_size("dp")
    planes = lax.axis_size("tensor")
    owned, width, rank = down.shape
    columns = up.shape[2]
    rows = groups * rows_local
    shape = jax.ShapeDtypeStruct

    (packed,) = call(
        functools.partial(pack_kernel, owned, planes),
        [shape((owners, groups, 2 * width + 128), BF16)],
        (index, tokens),
        [
            pltpu.VMEM((groups, rows_local, 2 * width), BF16),
            pltpu.VMEM(index.shape, I32),
            pltpu.SemaphoreType.DMA((4,)),
        ],
        in_hbm=(0, 1),
        vmem=62,
    )
    received = lax.all_to_all(packed, "dp", split_axis=0, concat_axis=0, tiled=True)

    down_own, up_own = down.transpose(0, 2, 1), up.reshape(owned * rank, columns)
    later, up_later, _ = lax.optimization_barrier((down_own, up_own, packed))
    upper, lower = later[:, :, width // 2 :], later[:, :, : width // 2]
    before = lax.ppermute(upper, "tensor", [(i, (i + 1) % planes) for i in range(planes)])
    after = lax.ppermute(lower, "tensor", [(i, (i - 1) % planes) for i in range(planes)])
    up_other = lax.ppermute(up_later, "dp", [(i, i ^ 1) for i in range(owners)])

    base = jnp.dot(tokens.reshape(rows, features), value_matrix, preferred_element_type=F32)
    (place,) = call(
        functools.partial(place_kernel, owned), [shape((rows, owners * 4), BF16)], (index,)
    )
    received, before, after, up_other, base, place = lax.optimization_barrier(
        (received, before, after, up_other, base, place)
    )
    partial, label = call(
        shrink_kernel,
        [shape((2 * planes, owners // 2, 128), BF16), shape((owners * 4, 128), BF16)],
        (received, before, down_own, after),
    )
    chips = [list(range(i, i + 2 * planes)) for i in range(0, owners * planes, 2 * planes)]
    partials = lax.all_to_all(
        partial, ("dp", "tensor"), split_axis=0, concat_axis=0, tiled=True, axis_index_groups=chips
    )
    (terms,) = call(
        expand_kernel,
        [shape((owners * 4, columns), BF16)],
        (partials, label, up_own, up_other),
    )
    arrived = lax.all_to_all(
        terms.reshape(owners // 2, 8, columns),
        "dp",
        split_axis=0,
        concat_axis=0,
        tiled=True,
        axis_index_groups=[list(range(core, owners, 2)) for core in range(2)],
    ).reshape(owners * 4, columns)
    (out,) = call(add_kernel, [shape((rows, columns), BF16)], (place, arrived, base))
    return out.reshape(groups, rows_local, columns)


def solution(mesh):
    in_specs = (
        P(None, "dp", None),
        P(None, "tensor"),
        P("dp", "tensor", None),
        P("dp", None, "tensor"),
        P(None, "dp"),
    )
    out_specs = P(None, "dp", "tensor")
    return jax.shard_map(
        on_device, mesh=mesh, in_specs=in_specs, out_specs=out_specs, check_vma=False
    )
```

```python
import functools

import jax
import jax.numpy as jnp
from jax import lax
from jax.experimental import pallas as pl
from jax.experimental.pallas import tpu as pltpu
from jax.sharding import PartitionSpec as P

BF16, F32, I32 = jnp.bfloat16, jnp.float32, jnp.int32
MIB = 1024 * 1024


def iota(shape, dim):
    return lax.broadcasted_iota(I32, shape, dim)


def read_index(index_ref, owned):
    along = jnp.concatenate([index_ref[0:1, :], index_ref[1:2, :]], axis=1)
    rows = along.shape[1]
    shift = owned.bit_length() - 1
    assert owned == 1 << shift
    key = (along >> shift) * 2 + jnp.where(iota((1, rows), 1) >= rows // 2, 1, 0)
    wide = jnp.broadcast_to(key, (rows, rows))
    line, column = iota((rows, rows), 0), iota((rows, rows), 1)
    same = jnp.sum(jnp.where(line == column, wide, 0).astype(F32), axis=1, keepdims=True)
    earlier = (wide.astype(F32) == same) & (line < column)
    place = jnp.sum(jnp.where(earlier, 1.0, 0.0), axis=0, keepdims=True)
    return wide, place, ((along & (owned - 1)) + 1).astype(F32)


def over_lanes(values):
    share = jnp.full((128, 128), 1.0 / 64.0, BF16)
    return jnp.dot(values.astype(BF16), share, preferred_element_type=F32)


def partner(plane, core, planes):
    step = (1 - 2 * (plane % 2)) * (1 - 2 * core)
    return (plane + step + planes) % planes


def pack_kernel(owned, planes, index_ref, tokens_ref, out_ref, held, pairs, indices, sems):
    width = held.shape[2]
    plane = lax.axis_index("tensor")
    parity = plane % 2

    def slice_of(plane):
        return tokens_ref.at[:, :, pl.ds(pl.multiple_of(plane * width, width), width)]

    copies = [
        pltpu.make_async_copy(index_ref, indices, sems.at[0]),
        pltpu.make_async_copy(slice_of(plane), held, sems.at[1]),
    ]
    for core in range(2):
        copies.append(
            pltpu.make_async_copy(
                slice_of(partner(plane, core, planes)), pairs.at[core], sems.at[2 + core]
            )
        )
    for copy in copies:
        copy.start()
    copies[0].wait()
    wide, place, label = read_index(indices, owned)
    rows = wide.shape[0]
    line, column = iota((rows, rows), 0), iota((rows, rows), 1)
    hit = line == wide
    label = jnp.broadcast_to(label, (rows, rows))
    labels = [
        jnp.sum(jnp.where(hit & (place == p), label, 0.0), axis=1, keepdims=True)
        for p in (0.0, 1.0)
    ]
    labels = jnp.where(column < 64, labels[0], labels[1]).astype(BF16)
    out_ref[:, :, 2 * width :] = labels.reshape(rows // 4, 4, 128)
    select = jnp.where(hit & (place == parity.astype(F32)), 1.0, 0.0)
    core = (line >> 1) & 1
    by_core = jnp.concatenate([jnp.where(core == c, select, 0.0) for c in range(2)], axis=1)
    copies[1].wait()
    packed = jnp.dot(
        select.astype(BF16), held[...].reshape(rows, width), preferred_element_type=F32
    )
    out_ref[:, :, :width] = packed.astype(BF16).reshape(rows // 4, 4, width)
    copies[2].wait()
    copies[3].wait()
    packed = jnp.dot(
        by_core.astype(BF16), pairs[...].reshape(2 * rows, width), preferred_element_type=F32
    )
    out_ref[:, :, width : 2 * width] = packed.astype(BF16).reshape(rows // 4, 4, width)


def shrink_kernel(
    received_ref, own_ref, own_pair_ref, other_ref, other_pair_ref, partial_ref, label_ref
):
    chips, per_chip, width = received_ref.shape
    width = (width - 128) // 2
    lines = chips * per_chip
    parity = lax.axis_index("tensor") % 2
    core = lax.axis_index("dp") % 2
    products = []
    for weights in ((own_ref, own_pair_ref), (other_ref, other_pair_ref)):
        product = None
        for e in range(2):
            mine = lax.dot_general(
                received_ref[:, :, e * width : (e + 1) * width].reshape(lines, width),
                weights[e][...].reshape(256, width),
                (((1,), (1,)), ((), ())),
                preferred_element_type=F32,
            )
            product = mine if e == 0 else product + mine
        products.append(product)
    own = (iota((lines, 256), 0) >> 1) & 1 == core
    product = jnp.where(own, products[0], products[1])
    label = received_ref[:, :, 2 * width :].reshape(lines, 128)
    upper = iota((lines, 128), 1) >> 6
    here = over_lanes(jnp.where(upper == parity, label.astype(F32), 0.0))
    upper = upper.astype(F32)
    total = jnp.where(here == upper + 1.0, product[:, :128], 0.0)
    total = total + jnp.where(here == upper + 3.0, product[:, 128:], 0.0)
    total = total + pltpu.roll(total, 64, 1)
    half = lines // 2
    packed = jnp.where(upper[:half] == 0.0, total[:half], total[half:]).astype(BF16)
    for peer in range(partial_ref.shape[0]):
        partial_ref[peer] = packed
    out_lines = label_ref.shape[0]
    line = iota((out_lines, lines), 0)
    source = (line >> 2) * 2 + (line & 1)
    take = jnp.where(iota((out_lines, lines), 1) == source, 1.0, 0.0).astype(BF16)
    label = jnp.dot(take, label, preferred_element_type=F32)
    line = iota((out_lines, 128), 0)
    label = over_lanes(jnp.where(iota((out_lines, 128), 1) >> 6 == (line >> 1) & 1, label, 0.0))
    other = (label > 0.0) & ((line >> 2) & 1 != core)
    label_ref[...] = jnp.where(other, label + 4.0, label).astype(BF16)


def expand_kernel(partial_ref, label_ref, up_own_ref, up_other_ref, out_ref):
    planes, half, _ = partial_ref.shape
    sums = []
    for p in range(2):
        total = partial_ref[p].astype(F32)
        for peer in range(p + 2, planes, 2):
            total = total + partial_ref[peer].astype(F32)
        sums.append(total.reshape(half // 8, 8, 128))
    spot = iota(sums[0].shape, 1) >> 1
    by_chip = []
    for chip in range(2):
        out = None
        for core in range(2):
            for p in range(2):
                by = (2 * core + 2 * p - 4 * chip) % 8
                piece = pltpu.roll(sums[p], by, 1) if by else sums[p]
                out = piece if out is None else jnp.where(spot == 2 * core + p, piece, out)
        by_chip.append(out)
    total = jnp.stack(by_chip, axis=1).reshape(half * 2, 128)
    turned = pltpu.roll(total, 64, 1)
    upper = iota(total.shape, 1) // 64
    lines = total.shape[0]
    for e in range(2):
        row = jnp.where(upper == e, total, turned)
        label = label_ref[e * lines : (e + 1) * lines].astype(F32)
        terms = None
        for up_ref, add in ((up_own_ref, 1.0), (up_other_ref, 5.0)):
            first = upper.astype(F32) + add
            left = jnp.where(label == first, row, 0.0)
            right = jnp.where(label == first + 2.0, row, 0.0)
            wide = jnp.concatenate([left, right], axis=1)
            high = wide.astype(BF16)
            for part in (high, (wide - high.astype(F32)).astype(BF16)):
                mine = jnp.dot(part, up_ref[...], preferred_element_type=F32)
                terms = mine if terms is None else terms + mine
        out_ref[e * lines : (e + 1) * lines] = terms.astype(BF16)


def place_kernel(owned, index_ref, out_ref):
    wide, place, _ = read_index(index_ref, owned)
    rows = wide.shape[0]
    key = wide[:1]
    target = (key >> 1) * 4 + place.astype(I32) * 2 + (key & 1)
    line, column = iota((rows, rows), 0), iota((rows, rows), 1)
    target = jnp.broadcast_to(target, (rows, rows))
    target = jnp.sum(jnp.where(line == column, target, 0).astype(F32), axis=1, keepdims=True)
    out_ref[...] = jnp.where(iota(out_ref.shape, 1).astype(F32) == target, 1.0, 0.0).astype(BF16)


def call(kernel, shapes, ins, scratch=(), in_hbm=(), vmem=40):
    nbytes = sum(v.size * v.dtype.itemsize for v in ins)

    def spec(hbm):
        return pl.BlockSpec(memory_space=pltpu.HBM if hbm else pltpu.VMEM)

    return pl.pallas_call(
        kernel,
        out_shape=shapes,
        in_specs=[spec(i in in_hbm) for i in range(len(ins))],
        out_specs=[spec(False) for _ in shapes],
        scratch_shapes=scratch,
        compiler_params=pltpu.CompilerParams(vmem_limit_bytes=vmem * MIB),
        cost_estimate=pl.CostEstimate(flops=0, bytes_accessed=nbytes, transcendentals=0),
    )(*ins)


def on_device(tokens, value_matrix, down, up, index):
    groups, rows_local, features = tokens.shape
    owners = lax.axis_size("dp")
    planes = lax.axis_size("tensor")
    owned, width, rank = down.shape
    columns = up.shape[2]
    rows = groups * rows_local
    shape = jax.ShapeDtypeStruct

    cores = 2
    same_core = [list(range(core, owners, cores)) for core in range(cores)]

    (packed,) = call(
        functools.partial(pack_kernel, owned, planes),
        [shape((owners // cores, cores * groups, 2 * width + 128), BF16)],
        (index, tokens),
        [
            pltpu.VMEM((groups, rows_local, width), BF16),
            pltpu.VMEM((cores, groups, rows_local, width), BF16),
            pltpu.VMEM(index.shape, I32),
            pltpu.SemaphoreType.DMA((4,)),
        ],
        in_hbm=(0, 1),
        vmem=62,
    )
    received = lax.all_to_all(
        packed, "dp", split_axis=0, concat_axis=0, tiled=True, axis_index_groups=same_core
    )

    def from_other_core(x):
        return lax.ppermute(x, "dp", [(i, i ^ 1) for i in range(owners)])

    down_own, up_own = down.transpose(0, 2, 1), up.reshape(owned * rank, columns)
    down_later, up_later, _ = lax.optimization_barrier((down_own, up_own, packed))
    pair_own = lax.ppermute(
        down_later,
        ("dp", "tensor"),
        [
            (i * planes + t, i * planes + partner(t, i % cores, planes))
            for i in range(owners)
            for t in range(planes)
        ],
    )
    down_other, up_other = from_other_core(down_later), from_other_core(up_later)
    pair_other = from_other_core(pair_own)

    base = jnp.dot(tokens.reshape(rows, features), value_matrix, preferred_element_type=F32)
    (place,) = call(
        functools.partial(place_kernel, owned), [shape((rows, owners * 4), BF16)], (index,)
    )
    received, pair_own, down_other, pair_other, up_other, base, place = lax.optimization_barrier(
        (received, pair_own, down_other, pair_other, up_other, base, place)
    )
    partial, label = call(
        shrink_kernel,
        [shape((planes, owners, 128), BF16), shape((owners * 4, 128), BF16)],
        (received, down_own, pair_own, down_other, pair_other),
    )
    partials = lax.all_to_all(partial, "tensor", split_axis=0, concat_axis=0, tiled=True)
    (terms,) = call(
        expand_kernel,
        [shape((owners * 4, columns), BF16)],
        (partials, label, up_own, up_other),
    )
    arrived = lax.all_to_all(
        terms.reshape(owners // cores, 4 * cores, columns),
        "dp",
        split_axis=0,
        concat_axis=0,
        tiled=True,
        axis_index_groups=same_core,
    ).reshape(owners * 4, columns)
    out = (base + jnp.dot(place, arrived, preferred_element_type=F32)).astype(BF16)
    return out.reshape(groups, rows_local, columns)


def solution(mesh):
    in_specs = (
        P(None, "dp", None),
        P(None, "tensor"),
        P("dp", "tensor", None),
        P("dp", None, "tensor"),
        P(None, "dp"),
    )
    out_specs = P(None, "dp", "tensor")
    return jax.shard_map(
        on_device, mesh=mesh, in_specs=in_specs, out_specs=out_specs, check_vma=False
    )
```

```python
import functools

import jax
import jax.numpy as jnp
from jax import lax
from jax.experimental import pallas as pl
from jax.experimental.pallas import tpu as pltpu
from jax.sharding import PartitionSpec as P

BF16, F32, I32 = jnp.bfloat16, jnp.float32, jnp.int32
MIB = 1024 * 1024


def iota(shape, dim):
    return lax.broadcasted_iota(I32, shape, dim)


def read_index(index_ref, owned):
    along = jnp.concatenate([index_ref[0:1, :], index_ref[1:2, :]], axis=1)
    rows = along.shape[1]
    shift = owned.bit_length() - 1
    assert owned == 1 << shift
    owner = along >> shift
    group = jnp.where(iota((1, rows), 1) >= rows // 2, 1, 0)
    wide = jnp.broadcast_to(owner * 2 + group, (rows, rows))
    line, column = iota((rows, rows), 0), iota((rows, rows), 1)
    same = jnp.sum(jnp.where(line == column, wide, 0).astype(F32), axis=1, keepdims=True)
    earlier = (wide.astype(F32) == same) & (line < column)
    place = jnp.sum(jnp.where(earlier, 1.0, 0.0), axis=0, keepdims=True).astype(I32)
    label = ((along & (owned - 1)) + 1).astype(F32)
    return (owner >> 1) * 4 + place * 2 + group, owner & 1, label


def over_lanes(values):
    share = jnp.full((128, 128), 1.0 / 64.0, BF16)
    return jnp.dot(values.astype(BF16), share, preferred_element_type=F32)


def partner(plane, core, planes):
    step = (1 - 2 * (plane % 2)) * (1 - 2 * core)
    return (plane + step + planes) % planes


def pack_kernel(owned, planes, index_ref, tokens_ref, out_ref, held, indices, sems):
    width = held.shape[2] // 2
    plane = lax.axis_index("tensor")
    core = lax.axis_index("dp") % 2
    copies = [pltpu.make_async_copy(index_ref, indices, sems.at[0])]
    for e, source in enumerate((plane, partner(plane, core, planes))):
        copies.append(
            pltpu.make_async_copy(
                tokens_ref.at[:, :, pl.ds(pl.multiple_of(source * width, width), width)],
                held.at[:, :, e * width : (e + 1) * width],
                sems.at[1 + e],
            )
        )
    for copy in copies:
        copy.start()
    copies[0].wait()
    target, owner_core, label = read_index(indices, owned)
    rows = target.shape[1]
    hit = iota((rows, rows), 0) == target
    labels = [
        jnp.sum(jnp.where(hit & (owner_core == c), label, 0.0), axis=1, keepdims=True)
        for c in range(2)
    ]
    labels = jnp.where(iota((rows, 128), 1) < 64, labels[0], labels[1]).astype(BF16)
    out_ref[:, :, 2 * width :] = labels.reshape(rows // 4, 4, 128)
    select = jnp.where(hit & (owner_core == plane % 2), 1.0, 0.0).astype(BF16)
    for copy in copies[1:]:
        copy.wait()
    tokens = held[...].reshape(rows, 2 * width)
    packed = jnp.dot(select, tokens, preferred_element_type=F32).astype(BF16)
    out_ref[:, :, : 2 * width] = packed.reshape(rows // 4, 4, 2 * width)


def shrink_kernel(
    received_ref, own_ref, first_ref, second_ref, partial_ref, label_ref, product_ref
):
    chips, per_chip, width = received_ref.shape
    width = (width - 128) // 2
    lines = chips * per_chip
    parity = lax.axis_index("tensor") % 2
    core = lax.axis_index("dp") % 2

    def multiply(weights):
        product = None
        for e in range(2):
            mine = lax.dot_general(
                received_ref[:, :, e * width : (e + 1) * width].reshape(lines, width),
                weights[e][...].reshape(256, width),
                (((1,), (1,)), ((), ())),
                preferred_element_type=F32,
            )
            product = mine if e == 0 else product + mine
        product_ref[...] = product

    @pl.when(core == parity)
    def _():
        multiply((own_ref, first_ref))

    @pl.when(core != parity)
    def _():
        multiply((first_ref, second_ref))

    label = received_ref[:, :, 2 * width :].reshape(lines, 128)
    upper = iota((lines, 128), 1) >> 6
    here = over_lanes(jnp.where(upper == parity, label.astype(F32), 0.0))
    upper = upper.astype(F32)
    total = jnp.where(here == upper + 1.0, product_ref[:, :128], 0.0)
    total = total + jnp.where(here == upper + 3.0, product_ref[:, 128:], 0.0)
    total = total + pltpu.roll(total, 64, 1)
    half = lines // 2
    packed = jnp.where(upper[:half] == 0.0, total[:half], total[half:]).astype(BF16)
    for peer in range(partial_ref.shape[0]):
        partial_ref[peer] = packed
    out_lines = label_ref.shape[0]
    line = iota((out_lines, lines), 0)
    source = (line >> 3) * 4 + (line & 3)
    take = jnp.where(iota((out_lines, lines), 1) == source, 1.0, 0.0).astype(BF16)
    label = jnp.dot(take, label, preferred_element_type=F32)
    line = iota((out_lines, 128), 0)
    label = over_lanes(jnp.where(iota((out_lines, 128), 1) >> 6 == (line >> 2) & 1, label, 0.0))
    other = (label > 0.0) & ((line >> 2) & 1 != core)
    label_ref[...] = jnp.where(other, label + 4.0, label).astype(BF16)


def expand_kernel(partial_ref, label_ref, up_own_ref, up_other_ref, out_ref):
    planes, half, _ = partial_ref.shape
    sums = []
    for p in range(2):
        total = partial_ref[p].astype(F32)
        for peer in range(p + 2, planes, 2):
            total = total + partial_ref[peer].astype(F32)
        sums.append(total.reshape(half // 8, 8, 128))
    first, second = sums
    low = iota(first.shape, 1) < 4
    by_chip = [
        jnp.where(low, first, pltpu.roll(second, 4, 1)),
        jnp.where(low, pltpu.roll(first, 4, 1), second),
    ]
    total = jnp.stack(by_chip, axis=1).reshape(half * 2, 128)
    turned = pltpu.roll(total, 64, 1)
    upper = iota(total.shape, 1) // 64
    lines = total.shape[0]
    for e in range(2):
        row = jnp.where(upper == e, total, turned)
        label = label_ref[e * lines : (e + 1) * lines].astype(F32)
        terms = None
        for up_ref, add in ((up_own_ref, 1.0), (up_other_ref, 5.0)):
            first = upper.astype(F32) + add
            left = jnp.where(label == first, row, 0.0)
            right = jnp.where(label == first + 2.0, row, 0.0)
            wide = jnp.concatenate([left, right], axis=1)
            high = wide.astype(BF16)
            for part in (high, (wide - high.astype(F32)).astype(BF16)):
                mine = jnp.dot(part, up_ref[...], preferred_element_type=F32)
                terms = mine if terms is None else terms + mine
        out_ref[e * lines : (e + 1) * lines] = terms.astype(BF16)


def place_kernel(owned, index_ref, out_ref):
    target, owner_core, _ = read_index(index_ref, owned)
    rows = target.shape[1]
    target = (target >> 2) * 8 + owner_core * 4 + (target & 3)
    line, column = iota((rows, rows), 0), iota((rows, rows), 1)
    target = jnp.broadcast_to(target, (rows, rows))
    target = jnp.sum(jnp.where(line == column, target, 0).astype(F32), axis=1, keepdims=True)
    out_ref[...] = jnp.where(iota(out_ref.shape, 1).astype(F32) == target, 1.0, 0.0).astype(BF16)


def call(kernel, shapes, ins, scratch=(), in_hbm=(), vmem=40):
    nbytes = sum(v.size * v.dtype.itemsize for v in ins)

    def spec(hbm):
        return pl.BlockSpec(memory_space=pltpu.HBM if hbm else pltpu.VMEM)

    return pl.pallas_call(
        kernel,
        out_shape=shapes,
        in_specs=[spec(i in in_hbm) for i in range(len(ins))],
        out_specs=[spec(False) for _ in shapes],
        scratch_shapes=scratch,
        compiler_params=pltpu.CompilerParams(vmem_limit_bytes=vmem * MIB),
        cost_estimate=pl.CostEstimate(flops=0, bytes_accessed=nbytes, transcendentals=0),
    )(*ins)


def on_device(tokens, value_matrix, down, up, index):
    groups, rows_local, features = tokens.shape
    owners = lax.axis_size("dp")
    planes = lax.axis_size("tensor")
    owned, width, rank = down.shape
    columns = up.shape[2]
    rows = groups * rows_local
    shape = jax.ShapeDtypeStruct

    cores = 2
    same_core = [list(range(core, owners, cores)) for core in range(cores)]

    (packed,) = call(
        functools.partial(pack_kernel, owned, planes),
        [shape((owners // cores, cores * groups, 2 * width + 128), BF16)],
        (index, tokens),
        [
            pltpu.VMEM((groups, rows_local, 2 * width), BF16),
            pltpu.VMEM(index.shape, I32),
            pltpu.SemaphoreType.DMA((3,)),
        ],
        in_hbm=(0, 1),
        vmem=62,
    )
    received = lax.all_to_all(
        packed, "dp", split_axis=0, concat_axis=0, tiled=True, axis_index_groups=same_core
    )

    down_own, up_own = down.transpose(0, 2, 1), up.reshape(owned * rank, columns)
    down_later, up_later, _ = lax.optimization_barrier((down_own, up_own, packed))
    first, second = [], []
    for i in range(owners):
        for t in range(planes):
            here, other = i * planes, (i ^ 1) * planes
            if i % cores == t % 2:
                first.append((here + t, other + t))
            else:
                first.append((here + t, here + (t - 1) % planes))
                second.append((here + t, other + (t + 1) % planes))
    down_first = lax.ppermute(down_later, ("dp", "tensor"), first)
    down_second = lax.ppermute(down_later, ("dp", "tensor"), second)
    up_other = lax.ppermute(up_later, "dp", [(i, i ^ 1) for i in range(owners)])

    base = jnp.dot(tokens.reshape(rows, features), value_matrix, preferred_element_type=F32)
    (place,) = call(
        functools.partial(place_kernel, owned), [shape((rows, owners * 4), BF16)], (index,)
    )
    received, down_first, down_second, up_other, base, place = lax.optimization_barrier(
        (received, down_first, down_second, up_other, base, place)
    )
    partial, label = call(
        shrink_kernel,
        [shape((planes, owners, 128), BF16), shape((owners * 4, 128), BF16)],
        (received, down_own, down_first, down_second),
        [pltpu.VMEM((rows, 256), F32)],
    )
    partials = lax.all_to_all(partial, "tensor", split_axis=0, concat_axis=0, tiled=True)
    (terms,) = call(
        expand_kernel,
        [shape((owners * 4, columns), BF16)],
        (partials, label, up_own, up_other),
    )
    arrived = lax.all_to_all(
        terms.reshape(owners // cores, 4 * cores, columns),
        "dp",
        split_axis=0,
        concat_axis=0,
        tiled=True,
        axis_index_groups=same_core,
    ).reshape(owners * 4, columns)
    out = (base + jnp.dot(place, arrived, preferred_element_type=F32)).astype(BF16)
    return out.reshape(groups, rows_local, columns)


def solution(mesh):
    in_specs = (
        P(None, "dp", None),
        P(None, "tensor"),
        P("dp", "tensor", None),
        P("dp", None, "tensor"),
        P(None, "dp"),
    )
    out_specs = P(None, "dp", "tensor")
    return jax.shard_map(
        on_device, mesh=mesh, in_specs=in_specs, out_specs=out_specs, check_vma=False
    )
```

```python
import functools

import jax
import jax.numpy as jnp
from jax import lax
from jax.experimental import pallas as pl
from jax.experimental.pallas import tpu as pltpu
from jax.sharding import PartitionSpec as P

BF16, F32, I32 = jnp.bfloat16, jnp.float32, jnp.int32
MIB = 1024 * 1024


def iota(shape, dim):
    return lax.broadcasted_iota(I32, shape, dim)


def read_index(index_ref, owned):
    along = jnp.concatenate([index_ref[0:1, :], index_ref[1:2, :]], axis=1)
    rows = along.shape[1]
    shift = owned.bit_length() - 1
    assert owned == 1 << shift
    owner = along >> shift
    group = jnp.where(iota((1, rows), 1) >= rows // 2, 1, 0)
    wide = jnp.broadcast_to(owner * 2 + group, (rows, rows))
    line, column = iota((rows, rows), 0), iota((rows, rows), 1)
    same = jnp.sum(jnp.where(line == column, wide, 0).astype(F32), axis=1, keepdims=True)
    earlier = (wide.astype(F32) == same) & (line < column)
    place = jnp.sum(jnp.where(earlier, 1.0, 0.0), axis=0, keepdims=True).astype(I32)
    label = ((along & (owned - 1)) + 1).astype(F32)
    return (owner >> 1) * 2 + group, place, owner & 1, label


def over_lanes(values):
    share = jnp.full((128, 128), 1.0 / 32.0, BF16)
    return jnp.dot(values.astype(BF16), share, preferred_element_type=F32)


def partner(plane, core, planes):
    step = (1 - 2 * (plane % 2)) * (1 - 2 * core)
    return (plane + step + planes) % planes


def pack_kernel(owned, planes, index_ref, tokens_ref, out_ref, held, indices, sems):
    width = held.shape[2] // 2
    plane = lax.axis_index("tensor")
    core = lax.axis_index("dp") % 2
    copies = [pltpu.make_async_copy(index_ref, indices, sems.at[0])]
    for e, source in enumerate((plane, partner(plane, core, planes))):
        copies.append(
            pltpu.make_async_copy(
                tokens_ref.at[:, :, pl.ds(pl.multiple_of(source * width, width), width)],
                held.at[:, :, e * width : (e + 1) * width],
                sems.at[1 + e],
            )
        )
    for copy in copies:
        copy.start()
    copies[0].wait()
    key, place, owner_core, label = read_index(indices, owned)
    rows, lines = key.shape[1], out_ref.shape[0] * out_ref.shape[1]
    hit = iota((2 * lines, rows), 0) == place * lines + key
    labels = None
    field = iota((lines, 128), 1) >> 5
    for c in range(2):
        found = jnp.where(hit & (owner_core == c), label, 0.0)
        found = jnp.sum(found, axis=1, keepdims=True)
        for p in range(2):
            mine = found[p * lines : (p + 1) * lines]
            labels = mine if labels is None else jnp.where(field == 2 * c + p, mine, labels)
    labels = jnp.broadcast_to(labels, (lines, 128)).astype(BF16)
    out_ref[:, :, 4 * width :] = labels.reshape(lines // 2, 2, 128)
    select = jnp.where(hit & (owner_core == plane % 2), 1.0, 0.0).astype(BF16)
    for copy in copies[1:]:
        copy.wait()
    tokens = held[...].reshape(rows, 2 * width)
    packed = jnp.dot(select, tokens, preferred_element_type=F32).astype(BF16)
    for p in range(2):
        out_ref[:, :, 2 * p * width : 2 * (p + 1) * width] = packed[
            p * lines : (p + 1) * lines
        ].reshape(lines // 2, 2, 2 * width)


def shrink(received_ref, weights, partial_ref, label_ref):
    chips, groups, width = received_ref.shape
    width = (width - 128) // 4
    lines = chips * groups
    parity = lax.axis_index("tensor") % 2
    core = lax.axis_index("dp") % 2

    def part(at):
        return received_ref[:, :, at * width : (at + 1) * width].reshape(lines, width)

    product = None
    for e in range(2):
        mine = lax.dot_general(
            jnp.concatenate([part(e), part(2 + e)], axis=0),
            weights[e][...].reshape(256, width),
            (((1,), (1,)), ((), ())),
            preferred_element_type=F32,
        )
        product = mine if e == 0 else product + mine
    label = received_ref[:, :, 4 * width :].reshape(lines, 128)
    field = iota((lines, 128), 1) >> 5
    here = [
        jnp.where(field == 2 * parity + p, label.astype(F32), 0.0) for p in range(2)
    ]
    here = over_lanes(jnp.concatenate(here, axis=0))
    upper = (iota((2 * lines, 128), 1) >> 6).astype(F32)
    total = jnp.where(here == upper + 1.0, product[:, :128], 0.0)
    total = total + jnp.where(here == upper + 3.0, product[:, 128:], 0.0)
    total = total + pltpu.roll(total, 64, 1)
    packed = jnp.where(upper[:lines] == 0.0, total[:lines], total[lines:]).astype(BF16)
    for peer in range(partial_ref.shape[0]):
        partial_ref[peer] = packed
    out_lines = label_ref.shape[0]
    line = iota((out_lines, lines), 0)
    source = (line >> 3) * 2 + (line & 1)
    take = jnp.where(iota((out_lines, lines), 1) == source, 1.0, 0.0).astype(BF16)
    label = jnp.dot(take, label, preferred_element_type=F32)
    line = iota((out_lines, 128), 0)
    label = over_lanes(jnp.where(iota((out_lines, 128), 1) >> 5 == (line >> 1) & 3, label, 0.0))
    other = (label > 0.0) & ((line >> 2) & 1 != core)
    label_ref[...] = jnp.where(other, label + 4.0, label).astype(BF16)


def shrink_kernel(received_ref, own_ref, first_ref, second_ref, partial_ref, label_ref):
    at_home = lax.axis_index("tensor") % 2 == lax.axis_index("dp") % 2

    @pl.when(at_home)
    def _():
        shrink(received_ref, (own_ref, first_ref), partial_ref, label_ref)

    @pl.when(jnp.logical_not(at_home))
    def _():
        shrink(received_ref, (first_ref, second_ref), partial_ref, label_ref)


def expand_kernel(partial_ref, label_ref, up_own_ref, up_other_ref, out_ref):
    planes, lines, _ = partial_ref.shape
    sums = []
    for q in range(2):
        total = partial_ref[q].astype(F32)
        for peer in range(q + 2, planes, 2):
            total = total + partial_ref[peer].astype(F32)
        sums.append(total.reshape(lines // 8, 8, 128))
    spot = iota(sums[0].shape, 1) >> 1
    by_chip = []
    for chip in range(4):
        out = None
        for field in range(4):
            by = 2 * (field - chip) % 8
            piece = pltpu.roll(sums[field // 2], by, 1) if by else sums[field // 2]
            out = piece if field == 0 else jnp.where(spot == field, piece, out)
        by_chip.append(out)
    total = jnp.stack(by_chip, axis=1).reshape(lines * 4, 128)
    upper = iota(total.shape, 1) >> 6
    place = (iota(total.shape, 0) >> 1) & 1
    row = jnp.where(upper == place, total, pltpu.roll(total, 64, 1))
    label = label_ref[...].astype(F32)
    terms = None
    for up_ref, add in ((up_own_ref, 1.0), (up_other_ref, 5.0)):
        at = upper.astype(F32) + add
        left = jnp.where(label == at, row, 0.0)
        right = jnp.where(label == at + 2.0, row, 0.0)
        wide = jnp.concatenate([left, right], axis=1)
        high = wide.astype(BF16)
        for part in (high, (wide - high.astype(F32)).astype(BF16)):
            mine = jnp.dot(part, up_ref[...], preferred_element_type=F32)
            terms = mine if terms is None else terms + mine
    out_ref[...] = terms.astype(BF16)


def place_kernel(owned, index_ref, out_ref):
    key, place, owner_core, _ = read_index(index_ref, owned)
    rows = key.shape[1]
    target = (key >> 1) * 8 + owner_core * 4 + place * 2 + (key & 1)
    line, column = iota((rows, rows), 0), iota((rows, rows), 1)
    target = jnp.broadcast_to(target, (rows, rows))
    target = jnp.sum(jnp.where(line == column, target, 0).astype(F32), axis=1, keepdims=True)
    out_ref[...] = jnp.where(iota(out_ref.shape, 1).astype(F32) == target, 1.0, 0.0).astype(BF16)


def call(kernel, shapes, ins, scratch=(), in_hbm=(), vmem=40):
    nbytes = sum(v.size * v.dtype.itemsize for v in ins)

    def spec(hbm):
        return pl.BlockSpec(memory_space=pltpu.HBM if hbm else pltpu.VMEM)

    return pl.pallas_call(
        kernel,
        out_shape=shapes,
        in_specs=[spec(i in in_hbm) for i in range(len(ins))],
        out_specs=[spec(False) for _ in shapes],
        scratch_shapes=scratch,
        compiler_params=pltpu.CompilerParams(vmem_limit_bytes=vmem * MIB),
        cost_estimate=pl.CostEstimate(flops=0, bytes_accessed=nbytes, transcendentals=0),
    )(*ins)


def on_device(tokens, value_matrix, down, up, index):
    groups, rows_local, features = tokens.shape
    owners = lax.axis_size("dp")
    planes = lax.axis_size("tensor")
    owned, width, rank = down.shape
    columns = up.shape[2]
    rows = groups * rows_local
    shape = jax.ShapeDtypeStruct

    cores = 2
    same_core = [list(range(core, owners, cores)) for core in range(cores)]

    (packed,) = call(
        functools.partial(pack_kernel, owned, planes),
        [shape((owners // cores, groups, 4 * width + 128), BF16)],
        (index, tokens),
        [
            pltpu.VMEM((groups, rows_local, 2 * width), BF16),
            pltpu.VMEM(index.shape, I32),
            pltpu.SemaphoreType.DMA((3,)),
        ],
        in_hbm=(0, 1),
        vmem=62,
    )
    received = lax.all_to_all(
        packed, "dp", split_axis=0, concat_axis=0, tiled=True, axis_index_groups=same_core
    )

    down_own, up_own = down.transpose(0, 2, 1), up.reshape(owned * rank, columns)
    down_later, up_later, _ = lax.optimization_barrier((down_own, up_own, packed))
    first, second = [], []
    for i in range(owners):
        for t in range(planes):
            here, other = i * planes, (i ^ 1) * planes
            if i % cores == t % 2:
                first.append((here + t, other + t))
            else:
                first.append((here + t, here + (t - 1) % planes))
                second.append((here + t, other + (t + 1) % planes))
    down_first = lax.ppermute(down_later, ("dp", "tensor"), first)
    down_second = lax.ppermute(down_later, ("dp", "tensor"), second)
    up_other = lax.ppermute(up_later, "dp", [(i, i ^ 1) for i in range(owners)])

    base = jnp.dot(tokens.reshape(rows, features), value_matrix, preferred_element_type=F32)
    (place,) = call(
        functools.partial(place_kernel, owned), [shape((rows, owners * 4), BF16)], (index,)
    )
    received, down_first, down_second, up_other, base, place = lax.optimization_barrier(
        (received, down_first, down_second, up_other, base, place)
    )
    partial, label = call(
        shrink_kernel,
        [shape((planes, owners, 128), BF16), shape((owners * 4, 128), BF16)],
        (received, down_own, down_first, down_second),
    )
    partials = lax.all_to_all(partial, "tensor", split_axis=0, concat_axis=0, tiled=True)
    (terms,) = call(
        expand_kernel,
        [shape((owners * 4, columns), BF16)],
        (partials, label, up_own, up_other),
    )
    arrived = lax.all_to_all(
        terms.reshape(owners // cores, 4 * cores, columns),
        "dp",
        split_axis=0,
        concat_axis=0,
        tiled=True,
        axis_index_groups=same_core,
    ).reshape(owners * 4, columns)
    out = (base + jnp.dot(place, arrived, preferred_element_type=F32)).astype(BF16)
    return out.reshape(groups, rows_local, columns)


def solution(mesh):
    in_specs = (
        P(None, "dp", None),
        P(None, "tensor"),
        P("dp", "tensor", None),
        P("dp", None, "tensor"),
        P(None, "dp"),
    )
    out_specs = P(None, "dp", "tensor")
    return jax.shard_map(
        on_device, mesh=mesh, in_specs=in_specs, out_specs=out_specs, check_vma=False
    )
```

```python
import functools

import jax
import jax.numpy as jnp
from jax import lax
from jax.experimental import pallas as pl
from jax.experimental.pallas import tpu as pltpu
from jax.sharding import PartitionSpec as P

BF16, F32, I32 = jnp.bfloat16, jnp.float32, jnp.int32
MIB = 1024 * 1024


def iota(shape, dim):
    return lax.broadcasted_iota(I32, shape, dim)


def read_index(index_ref, owned):
    along = jnp.concatenate([index_ref[0:1, :], index_ref[1:2, :]], axis=1)
    rows = along.shape[1]
    shift = owned.bit_length() - 1
    assert owned == 1 << shift
    owner = along >> shift
    group = jnp.where(iota((1, rows), 1) >= rows // 2, 1, 0)
    wide = jnp.broadcast_to(owner * 2 + group, (rows, rows))
    line, column = iota((rows, rows), 0), iota((rows, rows), 1)
    same = jnp.sum(jnp.where(line == column, wide, 0).astype(F32), axis=1, keepdims=True)
    earlier = (wide.astype(F32) == same) & (line < column)
    place = jnp.sum(jnp.where(earlier, 1.0, 0.0), axis=0, keepdims=True).astype(I32)
    label = ((along & (owned - 1)) + 1).astype(F32)
    return (owner >> 1) * 2 + group, place, owner & 1, label


def over_lanes(values):
    share = jnp.full((128, 128), 1.0 / 32.0, BF16)
    return jnp.dot(values.astype(BF16), share, preferred_element_type=F32)


def partner(plane, core, planes):
    step = (1 - 2 * (plane % 2)) * (1 - 2 * core)
    return (plane + step + planes) % planes


def pack_kernel(owned, planes, index_ref, tokens_ref, out_ref, held, indices, sems):
    width = held.shape[2] // 2
    plane = lax.axis_index("tensor")
    core = lax.axis_index("dp") % 2
    copies = [pltpu.make_async_copy(index_ref, indices, sems.at[0])]
    for e, source in enumerate((plane, partner(plane, core, planes))):
        copies.append(
            pltpu.make_async_copy(
                tokens_ref.at[:, :, pl.ds(pl.multiple_of(source * width, width), width)],
                held.at[:, :, e * width : (e + 1) * width],
                sems.at[1 + e],
            )
        )
    for copy in copies:
        copy.start()
    copies[0].wait()
    key, place, owner_core, label = read_index(indices, owned)
    rows, lines = key.shape[1], out_ref.shape[0] * out_ref.shape[1]
    hit = iota((2 * lines, rows), 0) == place * lines + key
    labels = None
    field = iota((lines, 128), 1) >> 5
    for c in range(2):
        found = jnp.where(hit & (owner_core == c), label, 0.0)
        found = jnp.sum(found, axis=1, keepdims=True)
        for p in range(2):
            mine = found[p * lines : (p + 1) * lines]
            labels = mine if labels is None else jnp.where(field == 2 * c + p, mine, labels)
    labels = jnp.broadcast_to(labels, (lines, 128)).astype(BF16)
    out_ref[:, :, 4 * width :] = labels.reshape(lines // 2, 2, 128)
    select = jnp.where(hit & (owner_core == plane % 2), 1.0, 0.0).astype(BF16)
    for copy in copies[1:]:
        copy.wait()
    tokens = held[...].reshape(rows, 2 * width)
    for e in range(2):
        part = tokens[:, e * width : (e + 1) * width]
        packed = jnp.dot(select, part, preferred_element_type=F32).astype(BF16)
        for p in range(2):
            at = (2 * p + e) * width
            out_ref[:, :, at : at + width] = packed[p * lines : (p + 1) * lines].reshape(
                lines // 2, 2, width
            )


def shrink(received_ref, weights, partial_ref, label_ref):
    chips, groups, width = received_ref.shape
    width = (width - 128) // 4
    lines = chips * groups
    parity = lax.axis_index("tensor") % 2
    core = lax.axis_index("dp") % 2

    def part(at):
        return received_ref[:, :, at * width : (at + 1) * width].reshape(lines, width)

    product = None
    for e in range(2):
        mine = lax.dot_general(
            jnp.concatenate([part(e), part(2 + e)], axis=0),
            weights[e][...],
            (((1,), (0,)), ((), ())),
            preferred_element_type=F32,
        )
        product = mine if e == 0 else product + mine
    label = received_ref[:, :, 4 * width :].reshape(lines, 128)
    field = iota((lines, 128), 1) >> 5
    here = [
        jnp.where(field == 2 * parity + p, label.astype(F32), 0.0) for p in range(2)
    ]
    here = over_lanes(jnp.concatenate(here, axis=0))
    upper = (iota((2 * lines, 128), 1) >> 6).astype(F32)
    total = jnp.where(here == upper + 1.0, product[:, :128], 0.0)
    total = total + jnp.where(here == upper + 3.0, product[:, 128:], 0.0)
    total = total + pltpu.roll(total, 64, 1)
    packed = jnp.where(upper[:lines] == 0.0, total[:lines], total[lines:]).astype(BF16)
    for peer in range(partial_ref.shape[0]):
        partial_ref[peer] = packed
    out_lines = label_ref.shape[0]
    line = iota((out_lines, lines), 0)
    source = (line >> 3) * 2 + (line & 1)
    take = jnp.where(iota((out_lines, lines), 1) == source, 1.0, 0.0).astype(BF16)
    label = jnp.dot(take, label, preferred_element_type=F32)
    line = iota((out_lines, 128), 0)
    label = over_lanes(jnp.where(iota((out_lines, 128), 1) >> 5 == (line >> 1) & 3, label, 0.0))
    other = (label > 0.0) & ((line >> 2) & 1 != core)
    label_ref[...] = jnp.where(other, label + 4.0, label).astype(BF16)


def shrink_kernel(received_ref, own_ref, first_ref, second_ref, partial_ref, label_ref):
    at_home = lax.axis_index("tensor") % 2 == lax.axis_index("dp") % 2

    @pl.when(at_home)
    def _():
        shrink(received_ref, (own_ref, first_ref), partial_ref, label_ref)

    @pl.when(jnp.logical_not(at_home))
    def _():
        shrink(received_ref, (first_ref, second_ref), partial_ref, label_ref)


def expand_kernel(partial_ref, label_ref, up_own_ref, up_other_ref, out_ref):
    planes, lines, _ = partial_ref.shape
    sums = []
    for q in range(2):
        total = partial_ref[q].astype(F32)
        for peer in range(q + 2, planes, 2):
            total = total + partial_ref[peer].astype(F32)
        sums.append(total.reshape(lines // 8, 8, 128))
    spot = iota(sums[0].shape, 1) >> 1
    by_chip = []
    for chip in range(4):
        out = None
        for field in range(4):
            by = 2 * (field - chip) % 8
            piece = pltpu.roll(sums[field // 2], by, 1) if by else sums[field // 2]
            out = piece if field == 0 else jnp.where(spot == field, piece, out)
        by_chip.append(out)
    total = jnp.stack(by_chip, axis=1).reshape(lines * 4, 128)
    upper = iota(total.shape, 1) >> 6
    place = (iota(total.shape, 0) >> 1) & 1
    row = jnp.where(upper == place, total, pltpu.roll(total, 64, 1))
    label = label_ref[...].astype(F32)
    terms = None
    for up_ref, add in ((up_own_ref, 1.0), (up_other_ref, 5.0)):
        at = upper.astype(F32) + add
        left = jnp.where(label == at, row, 0.0)
        right = jnp.where(label == at + 2.0, row, 0.0)
        wide = jnp.concatenate([left, right], axis=1)
        high = wide.astype(BF16)
        for part in (high, (wide - high.astype(F32)).astype(BF16)):
            mine = jnp.dot(part, up_ref[...], preferred_element_type=F32)
            terms = mine if terms is None else terms + mine
    out_ref[...] = terms.astype(BF16)


def place_kernel(owned, index_ref, out_ref):
    key, place, owner_core, _ = read_index(index_ref, owned)
    rows = key.shape[1]
    target = (key >> 1) * 8 + owner_core * 4 + place * 2 + (key & 1)
    line, column = iota((rows, rows), 0), iota((rows, rows), 1)
    target = jnp.broadcast_to(target, (rows, rows))
    target = jnp.sum(jnp.where(line == column, target, 0).astype(F32), axis=1, keepdims=True)
    out_ref[...] = jnp.where(iota(out_ref.shape, 1).astype(F32) == target, 1.0, 0.0).astype(BF16)


def call(kernel, shapes, ins, scratch=(), in_hbm=(), vmem=40):
    nbytes = sum(v.size * v.dtype.itemsize for v in ins)

    def spec(hbm):
        return pl.BlockSpec(memory_space=pltpu.HBM if hbm else pltpu.VMEM)

    return pl.pallas_call(
        kernel,
        out_shape=shapes,
        in_specs=[spec(i in in_hbm) for i in range(len(ins))],
        out_specs=[spec(False) for _ in shapes],
        scratch_shapes=scratch,
        compiler_params=pltpu.CompilerParams(vmem_limit_bytes=vmem * MIB),
        cost_estimate=pl.CostEstimate(flops=0, bytes_accessed=nbytes, transcendentals=0),
    )(*ins)


def on_device(tokens, value_matrix, down, up, index):
    groups, rows_local, features = tokens.shape
    owners = lax.axis_size("dp")
    planes = lax.axis_size("tensor")
    owned, width, rank = down.shape
    columns = up.shape[2]
    rows = groups * rows_local
    shape = jax.ShapeDtypeStruct

    cores = 2
    same_core = [list(range(core, owners, cores)) for core in range(cores)]

    (packed,) = call(
        functools.partial(pack_kernel, owned, planes),
        [shape((owners // cores, groups, 4 * width + 128), BF16)],
        (index, tokens),
        [
            pltpu.VMEM((groups, rows_local, 2 * width), BF16),
            pltpu.VMEM(index.shape, I32),
            pltpu.SemaphoreType.DMA((3,)),
        ],
        in_hbm=(0, 1),
        vmem=62,
    )
    received = lax.all_to_all(
        packed, "dp", split_axis=0, concat_axis=0, tiled=True, axis_index_groups=same_core
    )

    up_own = up.reshape(owned * rank, columns)
    down_later, up_later, _ = lax.optimization_barrier((down, up_own, packed))
    down_own = down_later.transpose(1, 0, 2).reshape(width, owned * rank)
    first, second = [], []
    for i in range(owners):
        for t in range(planes):
            here, other = i * planes, (i ^ 1) * planes
            if i % cores == t % 2:
                first.append((here + t, other + t))
            else:
                first.append((here + t, here + (t - 1) % planes))
                second.append((here + t, other + (t + 1) % planes))
    down_first = lax.ppermute(down_own, ("dp", "tensor"), first)
    down_second = lax.ppermute(down_own, ("dp", "tensor"), second)
    up_other = lax.ppermute(up_later, "dp", [(i, i ^ 1) for i in range(owners)])

    base = jnp.dot(tokens.reshape(rows, features), value_matrix, preferred_element_type=F32)
    (place,) = call(
        functools.partial(place_kernel, owned), [shape((rows, owners * 4), BF16)], (index,)
    )
    received, down_first, down_second, up_other, base, place = lax.optimization_barrier(
        (received, down_first, down_second, up_other, base, place)
    )
    partial, label = call(
        shrink_kernel,
        [shape((planes, owners, 128), BF16), shape((owners * 4, 128), BF16)],
        (received, down_own, down_first, down_second),
    )
    partials = lax.all_to_all(partial, "tensor", split_axis=0, concat_axis=0, tiled=True)
    (terms,) = call(
        expand_kernel,
        [shape((owners * 4, columns), BF16)],
        (partials, label, up_own, up_other),
    )
    arrived = lax.all_to_all(
        terms.reshape(owners // cores, 4 * cores, columns),
        "dp",
        split_axis=0,
        concat_axis=0,
        tiled=True,
        axis_index_groups=same_core,
    ).reshape(owners * 4, columns)
    out = (base + jnp.dot(place, arrived, preferred_element_type=F32)).astype(BF16)
    return out.reshape(groups, rows_local, columns)


def solution(mesh):
    in_specs = (
        P(None, "dp", None),
        P(None, "tensor"),
        P("dp", "tensor", None),
        P("dp", None, "tensor"),
        P(None, "dp"),
    )
    out_specs = P(None, "dp", "tensor")
    return jax.shard_map(
        on_device, mesh=mesh, in_specs=in_specs, out_specs=out_specs, check_vma=False
    )
```

```python
import functools

import jax
import jax.numpy as jnp
from jax import lax
from jax.experimental import pallas as pl
from jax.experimental.pallas import tpu as pltpu
from jax.sharding import PartitionSpec as P

BF16, F32, I32 = jnp.bfloat16, jnp.float32, jnp.int32
MIB = 1024 * 1024


def iota(shape, dim):
    return lax.broadcasted_iota(I32, shape, dim)


def read_index(index_ref, owned):
    along = jnp.concatenate([index_ref[0:1, :], index_ref[1:2, :]], axis=1)
    rows = along.shape[1]
    shift = owned.bit_length() - 1
    assert owned == 1 << shift
    owner = along >> shift
    group = jnp.where(iota((1, rows), 1) >= rows // 2, 1, 0)
    wide = jnp.broadcast_to(owner * 2 + group, (rows, rows))
    line, column = iota((rows, rows), 0), iota((rows, rows), 1)
    same = jnp.sum(jnp.where(line == column, wide, 0).astype(F32), axis=1, keepdims=True)
    earlier = (wide.astype(F32) == same) & (line < column)
    place = jnp.sum(jnp.where(earlier, 1.0, 0.0), axis=0, keepdims=True).astype(I32)
    label = ((along & (owned - 1)) + 1).astype(F32)
    return (owner >> 1) * 2 + group, place, owner & 1, label


def over_lanes(values):
    share = jnp.full((128, 128), 1.0 / 32.0, BF16)
    return jnp.dot(values.astype(BF16), share, preferred_element_type=F32)


def partner(plane, core, planes):
    step = (1 - 2 * (plane % 2)) * (1 - 2 * core)
    return (plane + step + planes) % planes


def pack_kernel(owned, planes, index_ref, tokens_ref, out_ref, held, indices, sems):
    width = held.shape[2] // 2
    plane = lax.axis_index("tensor")
    core = lax.axis_index("dp") % 2
    copies = [pltpu.make_async_copy(index_ref, indices, sems.at[0])]
    for e, source in enumerate((plane, partner(plane, core, planes))):
        copies.append(
            pltpu.make_async_copy(
                tokens_ref.at[:, :, pl.ds(pl.multiple_of(source * width, width), width)],
                held.at[:, :, e * width : (e + 1) * width],
                sems.at[1 + e],
            )
        )
    for copy in copies:
        copy.start()
    copies[0].wait()
    key, place, owner_core, label = read_index(indices, owned)
    rows, lines = key.shape[1], out_ref.shape[0] * out_ref.shape[1]
    hit = iota((2 * lines, rows), 0) == place * lines + key
    labels = None
    field = iota((lines, 128), 1) >> 5
    for c in range(2):
        found = jnp.where(hit & (owner_core == c), label, 0.0)
        found = jnp.sum(found, axis=1, keepdims=True)
        for p in range(2):
            mine = found[p * lines : (p + 1) * lines]
            labels = mine if labels is None else jnp.where(field == 2 * c + p, mine, labels)
    labels = jnp.broadcast_to(labels, (lines, 128)).astype(BF16)
    out_ref[:, :, 4 * width :] = labels.reshape(lines // 2, 2, 128)
    select = jnp.where(hit & (owner_core == plane % 2), 1.0, 0.0).astype(BF16)
    for copy in copies[1:]:
        copy.wait()
    tokens = held[...].reshape(rows, 2 * width)
    for e in range(2):
        part = tokens[:, e * width : (e + 1) * width]
        packed = jnp.dot(select, part, preferred_element_type=F32).astype(BF16)
        for p in range(2):
            at = (2 * p + e) * width
            out_ref[:, :, at : at + width] = packed[p * lines : (p + 1) * lines].reshape(
                lines // 2, 2, width
            )


def shrink(received_ref, weights, partial_ref, label_ref):
    chips, groups, width = received_ref.shape
    width = (width - 128) // 4
    lines = chips * groups
    parity = lax.axis_index("tensor") % 2
    core = lax.axis_index("dp") % 2

    def part(at):
        return received_ref[:, :, at * width : (at + 1) * width].reshape(lines, width)

    product = None
    for e in range(2):
        mine = lax.dot_general(
            jnp.concatenate([part(e), part(2 + e)], axis=0),
            weights[e][...],
            (((1,), (0,)), ((), ())),
            preferred_element_type=F32,
        )
        product = mine if e == 0 else product + mine
    label = received_ref[:, :, 4 * width :].reshape(lines, 128)
    field = iota((lines, 128), 1) >> 5
    here = [
        jnp.where(field == 2 * parity + p, label.astype(F32), 0.0) for p in range(2)
    ]
    here = jnp.concatenate(here, axis=0)
    here = here + pltpu.roll(here, 64, 1)
    here = here + pltpu.roll(here, 32, 1)
    upper = (iota((2 * lines, 128), 1) >> 6).astype(F32)
    total = jnp.where(here == upper + 1.0, product[:, :128], 0.0)
    total = total + jnp.where(here == upper + 3.0, product[:, 128:], 0.0)
    total = total + pltpu.roll(total, 64, 1)
    packed = jnp.where(upper[:lines] == 0.0, total[:lines], total[lines:]).astype(BF16)
    for peer in range(partial_ref.shape[0]):
        partial_ref[peer] = packed
    out_lines = label_ref.shape[0]
    line = iota((out_lines, lines), 0)
    source = (line >> 3) * 2 + (line & 1)
    take = jnp.where(iota((out_lines, lines), 1) == source, 1.0, 0.0).astype(BF16)
    label = jnp.dot(take, label, preferred_element_type=F32)
    line = iota((out_lines, 128), 0)
    label = over_lanes(jnp.where(iota((out_lines, 128), 1) >> 5 == (line >> 1) & 3, label, 0.0))
    other = (label > 0.0) & ((line >> 2) & 1 != core)
    label_ref[...] = jnp.where(other, label + 4.0, label).astype(BF16)


def shrink_kernel(received_ref, own_ref, first_ref, second_ref, partial_ref, label_ref):
    at_home = lax.axis_index("tensor") % 2 == lax.axis_index("dp") % 2

    @pl.when(at_home)
    def _():
        shrink(received_ref, (own_ref, first_ref), partial_ref, label_ref)

    @pl.when(jnp.logical_not(at_home))
    def _():
        shrink(received_ref, (first_ref, second_ref), partial_ref, label_ref)


def expand_kernel(partial_ref, label_ref, up_own_ref, up_other_ref, out_ref):
    planes, lines, _ = partial_ref.shape
    sums = []
    for q in range(2):
        total = partial_ref[q].astype(F32)
        for peer in range(q + 2, planes, 2):
            total = total + partial_ref[peer].astype(F32)
        sums.append(total.reshape(lines // 8, 8, 128))
    spot = iota(sums[0].shape, 1) >> 1
    by_chip = []
    for chip in range(4):
        out = None
        for field in range(4):
            by = 2 * (field - chip) % 8
            piece = pltpu.roll(sums[field // 2], by, 1) if by else sums[field // 2]
            out = piece if field == 0 else jnp.where(spot == field, piece, out)
        by_chip.append(out)
    total = jnp.stack(by_chip, axis=1).reshape(lines * 4, 128)
    upper = iota(total.shape, 1) >> 6
    place = (iota(total.shape, 0) >> 1) & 1
    row = jnp.where(upper == place, total, pltpu.roll(total, 64, 1))
    label = label_ref[...].astype(F32)
    terms = None
    for up_ref, add in ((up_own_ref, 1.0), (up_other_ref, 5.0)):
        at = upper.astype(F32) + add
        left = jnp.where(label == at, row, 0.0)
        right = jnp.where(label == at + 2.0, row, 0.0)
        wide = jnp.concatenate([left, right], axis=1).astype(BF16)
        mine = jnp.dot(wide, up_ref[...], preferred_element_type=F32)
        terms = mine if terms is None else terms + mine
    out_ref[...] = terms.astype(BF16)


def place_kernel(owned, index_ref, out_ref):
    key, place, owner_core, _ = read_index(index_ref, owned)
    rows = key.shape[1]
    target = (key >> 1) * 8 + owner_core * 4 + place * 2 + (key & 1)
    line, column = iota((rows, rows), 0), iota((rows, rows), 1)
    target = jnp.broadcast_to(target, (rows, rows))
    target = jnp.sum(jnp.where(line == column, target, 0).astype(F32), axis=1, keepdims=True)
    out_ref[...] = jnp.where(iota(out_ref.shape, 1).astype(F32) == target, 1.0, 0.0).astype(BF16)


def call(kernel, shapes, ins, scratch=(), in_hbm=(), vmem=40):
    nbytes = sum(v.size * v.dtype.itemsize for v in ins)

    def spec(hbm):
        return pl.BlockSpec(memory_space=pltpu.HBM if hbm else pltpu.VMEM)

    return pl.pallas_call(
        kernel,
        out_shape=shapes,
        in_specs=[spec(i in in_hbm) for i in range(len(ins))],
        out_specs=[spec(False) for _ in shapes],
        scratch_shapes=scratch,
        compiler_params=pltpu.CompilerParams(vmem_limit_bytes=vmem * MIB),
        cost_estimate=pl.CostEstimate(flops=0, bytes_accessed=nbytes, transcendentals=0),
    )(*ins)


def on_device(tokens, value_matrix, down, up, index):
    groups, rows_local, features = tokens.shape
    owners = lax.axis_size("dp")
    planes = lax.axis_size("tensor")
    owned, width, rank = down.shape
    columns = up.shape[2]
    rows = groups * rows_local
    shape = jax.ShapeDtypeStruct

    cores = 2
    same_core = [list(range(core, owners, cores)) for core in range(cores)]

    (packed,) = call(
        functools.partial(pack_kernel, owned, planes),
        [shape((owners // cores, groups, 4 * width + 128), BF16)],
        (index, tokens),
        [
            pltpu.VMEM((groups, rows_local, 2 * width), BF16),
            pltpu.VMEM(index.shape, I32),
            pltpu.SemaphoreType.DMA((3,)),
        ],
        in_hbm=(0, 1),
        vmem=62,
    )
    received = lax.all_to_all(
        packed, "dp", split_axis=0, concat_axis=0, tiled=True, axis_index_groups=same_core
    )

    up_own = up.reshape(owned * rank, columns)
    down_later, up_later, _ = lax.optimization_barrier((down, up_own, packed))
    down_own = down_later.transpose(1, 0, 2).reshape(width, owned * rank)
    first, second = [], []
    for i in range(owners):
        for t in range(planes):
            here, other = i * planes, (i ^ 1) * planes
            if i % cores == t % 2:
                first.append((here + t, other + t))
            else:
                first.append((here + t, here + (t - 1) % planes))
                second.append((here + t, other + (t + 1) % planes))
    down_first = lax.ppermute(down_own, ("dp", "tensor"), first)
    down_second = lax.ppermute(down_own, ("dp", "tensor"), second)
    up_other = lax.ppermute(up_later, "dp", [(i, i ^ 1) for i in range(owners)])

    base = jnp.dot(tokens.reshape(rows, features), value_matrix, preferred_element_type=F32)
    (place,) = call(
        functools.partial(place_kernel, owned), [shape((rows, owners * 4), BF16)], (index,)
    )
    received, down_first, down_second, up_other, base, place = lax.optimization_barrier(
        (received, down_first, down_second, up_other, base, place)
    )
    partial, label = call(
        shrink_kernel,
        [shape((planes, owners, 128), BF16), shape((owners * 4, 128), BF16)],
        (received, down_own, down_first, down_second),
    )
    partials = lax.all_to_all(partial, "tensor", split_axis=0, concat_axis=0, tiled=True)
    (terms,) = call(
        expand_kernel,
        [shape((owners * 4, columns), BF16)],
        (partials, label, up_own, up_other),
    )
    arrived = lax.all_to_all(
        terms.reshape(owners // cores, 4 * cores, columns),
        "dp",
        split_axis=0,
        concat_axis=0,
        tiled=True,
        axis_index_groups=same_core,
    ).reshape(owners * 4, columns)
    out = (base + jnp.dot(place, arrived, preferred_element_type=F32)).astype(BF16)
    return out.reshape(groups, rows_local, columns)


def solution(mesh):
    in_specs = (
        P(None, "dp", None),
        P(None, "tensor"),
        P("dp", "tensor", None),
        P("dp", None, "tensor"),
        P(None, "dp"),
    )
    out_specs = P(None, "dp", "tensor")
    return jax.shard_map(
        on_device, mesh=mesh, in_specs=in_specs, out_specs=out_specs, check_vma=False
    )
```

```python
import functools

import jax
import jax.numpy as jnp
from jax import lax
from jax.experimental import pallas as pl
from jax.experimental.pallas import tpu as pltpu
from jax.sharding import PartitionSpec as P

BF16, F32, I32 = jnp.bfloat16, jnp.float32, jnp.int32
MIB = 1024 * 1024


def iota(shape, dim):
    return lax.broadcasted_iota(I32, shape, dim)


def read_index(index_ref, owned):
    along = jnp.concatenate([index_ref[0:1, :], index_ref[1:2, :]], axis=1)
    rows = along.shape[1]
    shift = owned.bit_length() - 1
    assert owned == 1 << shift
    owner = along >> shift
    group = jnp.where(iota((1, rows), 1) >= rows // 2, 1, 0)
    wide = jnp.broadcast_to(owner * 2 + group, (rows, rows))
    line, column = iota((rows, rows), 0), iota((rows, rows), 1)
    same = jnp.sum(jnp.where(line == column, wide, 0).astype(F32), axis=1, keepdims=True)
    earlier = (wide.astype(F32) == same) & (line < column)
    place = jnp.sum(jnp.where(earlier, 1.0, 0.0), axis=0, keepdims=True).astype(I32)
    label = ((along & (owned - 1)) + 1).astype(F32)
    return (owner >> 1) * 2 + group, place, owner & 1, label


def over_lanes(values):
    share = jnp.full((128, 128), 1.0 / 32.0, BF16)
    return jnp.dot(values.astype(BF16), share, preferred_element_type=F32)


def partner(plane, core, planes):
    step = (1 - 2 * (plane % 2)) * (1 - 2 * core)
    return (plane + step + planes) % planes


def pack_kernel(owned, planes, index_ref, tokens_ref, out_ref, held, indices, sems):
    width = held.shape[2] // 2
    plane = lax.axis_index("tensor")
    core = lax.axis_index("dp") % 2
    copies = [pltpu.make_async_copy(index_ref, indices, sems.at[0])]
    for e, source in enumerate((plane, partner(plane, core, planes))):
        copies.append(
            pltpu.make_async_copy(
                tokens_ref.at[:, :, pl.ds(pl.multiple_of(source * width, width), width)],
                held.at[:, :, e * width : (e + 1) * width],
                sems.at[1 + e],
            )
        )
    for copy in copies:
        copy.start(priority=1)
    copies[0].wait()
    key, place, owner_core, label = read_index(indices, owned)
    rows, lines = key.shape[1], out_ref.shape[0] * out_ref.shape[1]
    hit = iota((2 * lines, rows), 0) == place * lines + key
    labels = None
    field = iota((lines, 128), 1) >> 5
    for c in range(2):
        found = jnp.where(hit & (owner_core == c), label, 0.0)
        found = jnp.sum(found, axis=1, keepdims=True)
        for p in range(2):
            mine = found[p * lines : (p + 1) * lines]
            labels = mine if labels is None else jnp.where(field == 2 * c + p, mine, labels)
    labels = jnp.broadcast_to(labels, (lines, 128)).astype(BF16)
    out_ref[:, :, 4 * width :] = labels.reshape(lines // 2, 2, 128)
    select = jnp.where(hit & (owner_core == plane % 2), 1.0, 0.0).astype(BF16)
    for copy in copies[1:]:
        copy.wait()
    tokens = held[...].reshape(rows, 2 * width)
    for e in range(2):
        part = tokens[:, e * width : (e + 1) * width]
        packed = jnp.dot(select, part, preferred_element_type=F32).astype(BF16)
        for p in range(2):
            at = (2 * p + e) * width
            out_ref[:, :, at : at + width] = packed[p * lines : (p + 1) * lines].reshape(
                lines // 2, 2, width
            )


def shrink(received_ref, weights, partial_ref, label_ref):
    chips, groups, width = received_ref.shape
    width = (width - 128) // 4
    lines = chips * groups
    parity = lax.axis_index("tensor") % 2
    core = lax.axis_index("dp") % 2

    def part(at):
        return received_ref[:, :, at * width : (at + 1) * width].reshape(lines, width)

    product = None
    for e in range(2):
        mine = lax.dot_general(
            jnp.concatenate([part(e), part(2 + e)], axis=0),
            weights[e][...],
            (((1,), (0,)), ((), ())),
            preferred_element_type=F32,
        )
        product = mine if e == 0 else product + mine
    label = received_ref[:, :, 4 * width :].reshape(lines, 128)
    field = iota((lines, 128), 1) >> 5
    here = [
        jnp.where(field == 2 * parity + p, label.astype(F32), 0.0) for p in range(2)
    ]
    here = jnp.concatenate(here, axis=0)
    here = here + pltpu.roll(here, 64, 1)
    here = here + pltpu.roll(here, 32, 1)
    upper = (iota((2 * lines, 128), 1) >> 6).astype(F32)
    total = jnp.where(here == upper + 1.0, product[:, :128], 0.0)
    total = total + jnp.where(here == upper + 3.0, product[:, 128:], 0.0)
    total = total + pltpu.roll(total, 64, 1)
    packed = jnp.where(upper[:lines] == 0.0, total[:lines], total[lines:]).astype(BF16)
    for peer in range(partial_ref.shape[0]):
        partial_ref[peer] = packed
    out_lines = label_ref.shape[0]
    line = iota((out_lines, lines), 0)
    source = (line >> 3) * 2 + (line & 1)
    take = jnp.where(iota((out_lines, lines), 1) == source, 1.0, 0.0).astype(BF16)
    label = jnp.dot(take, label, preferred_element_type=F32)
    line = iota((out_lines, 128), 0)
    label = over_lanes(jnp.where(iota((out_lines, 128), 1) >> 5 == (line >> 1) & 3, label, 0.0))
    other = (label > 0.0) & ((line >> 2) & 1 != core)
    label_ref[...] = jnp.where(other, label + 4.0, label).astype(BF16)


def shrink_kernel(received_ref, own_ref, first_ref, second_ref, partial_ref, label_ref):
    at_home = lax.axis_index("tensor") % 2 == lax.axis_index("dp") % 2

    @pl.when(at_home)
    def _():
        shrink(received_ref, (own_ref, first_ref), partial_ref, label_ref)

    @pl.when(jnp.logical_not(at_home))
    def _():
        shrink(received_ref, (first_ref, second_ref), partial_ref, label_ref)


def expand_kernel(partial_ref, label_ref, up_own_ref, up_other_ref, out_ref):
    planes, lines, _ = partial_ref.shape
    sums = []
    for q in range(2):
        total = partial_ref[q].astype(F32)
        for peer in range(q + 2, planes, 2):
            total = total + partial_ref[peer].astype(F32)
        sums.append(total.reshape(lines // 8, 8, 128))
    spot = iota(sums[0].shape, 1) >> 1
    by_chip = []
    for chip in range(4):
        out = None
        for field in range(4):
            by = 2 * (field - chip) % 8
            piece = pltpu.roll(sums[field // 2], by, 1) if by else sums[field // 2]
            out = piece if field == 0 else jnp.where(spot == field, piece, out)
        by_chip.append(out)
    total = jnp.stack(by_chip, axis=1).reshape(lines * 4, 128)
    upper = iota(total.shape, 1) >> 6
    place = (iota(total.shape, 0) >> 1) & 1
    row = jnp.where(upper == place, total, pltpu.roll(total, 64, 1))
    label = label_ref[...].astype(F32)
    terms = None
    for up_ref, add in ((up_own_ref, 1.0), (up_other_ref, 5.0)):
        at = upper.astype(F32) + add
        left = jnp.where(label == at, row, 0.0)
        right = jnp.where(label == at + 2.0, row, 0.0)
        wide = jnp.concatenate([left, right], axis=1).astype(BF16)
        mine = jnp.dot(wide, up_ref[...], preferred_element_type=F32)
        terms = mine if terms is None else terms + mine
    out_ref[...] = terms.astype(BF16)


def place_kernel(owned, index_ref, out_ref):
    key, place, owner_core, _ = read_index(index_ref, owned)
    rows = key.shape[1]
    target = (key >> 1) * 8 + owner_core * 4 + place * 2 + (key & 1)
    line, column = iota((rows, rows), 0), iota((rows, rows), 1)
    target = jnp.broadcast_to(target, (rows, rows))
    target = jnp.sum(jnp.where(line == column, target, 0).astype(F32), axis=1, keepdims=True)
    out_ref[...] = jnp.where(iota(out_ref.shape, 1).astype(F32) == target, 1.0, 0.0).astype(BF16)


def call(kernel, shapes, ins, scratch=(), in_hbm=(), vmem=40):
    nbytes = sum(v.size * v.dtype.itemsize for v in ins)

    def spec(hbm):
        return pl.BlockSpec(memory_space=pltpu.HBM if hbm else pltpu.VMEM)

    return pl.pallas_call(
        kernel,
        out_shape=shapes,
        in_specs=[spec(i in in_hbm) for i in range(len(ins))],
        out_specs=[spec(False) for _ in shapes],
        scratch_shapes=scratch,
        compiler_params=pltpu.CompilerParams(vmem_limit_bytes=vmem * MIB),
        cost_estimate=pl.CostEstimate(flops=0, bytes_accessed=nbytes, transcendentals=0),
    )(*ins)


def on_device(tokens, value_matrix, down, up, index):
    groups, rows_local, features = tokens.shape
    owners = lax.axis_size("dp")
    planes = lax.axis_size("tensor")
    owned, width, rank = down.shape
    columns = up.shape[2]
    rows = groups * rows_local
    shape = jax.ShapeDtypeStruct

    cores = 2
    same_core = [list(range(core, owners, cores)) for core in range(cores)]

    (packed,) = call(
        functools.partial(pack_kernel, owned, planes),
        [shape((owners // cores, groups, 4 * width + 128), BF16)],
        (index, tokens),
        [
            pltpu.VMEM((groups, rows_local, 2 * width), BF16),
            pltpu.VMEM(index.shape, I32),
            pltpu.SemaphoreType.DMA((3,)),
        ],
        in_hbm=(0, 1),
        vmem=62,
    )
    received = lax.all_to_all(
        packed, "dp", split_axis=0, concat_axis=0, tiled=True, axis_index_groups=same_core
    )

    up_own = up.reshape(owned * rank, columns)
    down_later, up_later, _ = lax.optimization_barrier((down, up_own, packed))
    down_own = down_later.transpose(1, 0, 2).reshape(width, owned * rank)
    first, second = [], []
    for i in range(owners):
        for t in range(planes):
            here, other = i * planes, (i ^ 1) * planes
            if i % cores == t % 2:
                first.append((here + t, other + t))
            else:
                first.append((here + t, here + (t - 1) % planes))
                second.append((here + t, other + (t + 1) % planes))
    down_first = lax.ppermute(down_own, ("dp", "tensor"), first)
    down_second = lax.ppermute(down_own, ("dp", "tensor"), second)
    up_other = lax.ppermute(up_later, "dp", [(i, i ^ 1) for i in range(owners)])

    base = jnp.dot(tokens.reshape(rows, features), value_matrix, preferred_element_type=F32)
    (place,) = call(
        functools.partial(place_kernel, owned), [shape((rows, owners * 4), BF16)], (index,)
    )
    received, down_first, down_second, up_other, base, place = lax.optimization_barrier(
        (received, down_first, down_second, up_other, base, place)
    )
    partial, label = call(
        shrink_kernel,
        [shape((planes, owners, 128), BF16), shape((owners * 4, 128), BF16)],
        (received, down_own, down_first, down_second),
    )
    partials = lax.all_to_all(partial, "tensor", split_axis=0, concat_axis=0, tiled=True)
    (terms,) = call(
        expand_kernel,
        [shape((owners * 4, columns), BF16)],
        (partials, label, up_own, up_other),
    )
    arrived = lax.all_to_all(
        terms.reshape(owners // cores, 4 * cores, columns),
        "dp",
        split_axis=0,
        concat_axis=0,
        tiled=True,
        axis_index_groups=same_core,
    ).reshape(owners * 4, columns)
    out = (base + jnp.dot(place, arrived, preferred_element_type=F32)).astype(BF16)
    return out.reshape(groups, rows_local, columns)


def solution(mesh):
    in_specs = (
        P(None, "dp", None),
        P(None, "tensor"),
        P("dp", "tensor", None),
        P("dp", None, "tensor"),
        P(None, "dp"),
    )
    out_specs = P(None, "dp", "tensor")
    return jax.shard_map(
        on_device, mesh=mesh, in_specs=in_specs, out_specs=out_specs, check_vma=False
    )
```

```python
import functools

import jax
import jax.numpy as jnp
from jax import lax
from jax.experimental import pallas as pl
from jax.experimental.pallas import tpu as pltpu
from jax.sharding import PartitionSpec as P

BF16, F32, I32 = jnp.bfloat16, jnp.float32, jnp.int32
MIB = 1024 * 1024


def iota(shape, dim):
    return lax.broadcasted_iota(I32, shape, dim)


def read_index(index_ref, owned):
    along = jnp.concatenate([index_ref[0:1, :], index_ref[1:2, :]], axis=1)
    rows = along.shape[1]
    shift = owned.bit_length() - 1
    assert owned == 1 << shift
    owner = along >> shift
    group = jnp.where(iota((1, rows), 1) >= rows // 2, 1, 0)
    wide = jnp.broadcast_to(owner * 2 + group, (rows, rows))
    line, column = iota((rows, rows), 0), iota((rows, rows), 1)
    same = jnp.sum(jnp.where(line == column, wide, 0).astype(F32), axis=1, keepdims=True)
    earlier = (wide.astype(F32) == same) & (line < column)
    place = jnp.sum(jnp.where(earlier, 1.0, 0.0), axis=0, keepdims=True).astype(I32)
    label = ((along & (owned - 1)) + 1).astype(F32)
    return (owner >> 1) * 2 + group, place, owner & 1, label


def over_lanes(values):
    share = jnp.full((128, 128), 1.0 / 32.0, BF16)
    return jnp.dot(values.astype(BF16), share, preferred_element_type=F32)


def partner(plane, core, planes):
    step = (1 - 2 * (plane % 2)) * (1 - 2 * core)
    return (plane + step + planes) % planes


def pack_kernel(owned, planes, index_ref, tokens_ref, out_ref, held, indices, sems):
    width = held.shape[2] // 2
    plane = lax.axis_index("tensor")
    core = lax.axis_index("dp") % 2
    copies = [pltpu.make_async_copy(index_ref, indices, sems.at[0])]
    for e, source in enumerate((plane, partner(plane, core, planes))):
        copies.append(
            pltpu.make_async_copy(
                tokens_ref.at[:, :, pl.ds(pl.multiple_of(source * width, width), width)],
                held.at[:, :, e * width : (e + 1) * width],
                sems.at[1 + e],
            )
        )
    for copy in copies:
        copy.start(priority=1)
    copies[0].wait()
    key, place, owner_core, label = read_index(indices, owned)
    rows, lines = key.shape[1], out_ref.shape[0] * out_ref.shape[1]
    hit = iota((2 * lines, rows), 0) == place * lines + key
    labels = None
    field = iota((lines, 128), 1) >> 5
    for c in range(2):
        found = jnp.where(hit & (owner_core == c), label, 0.0)
        found = jnp.sum(found, axis=1, keepdims=True)
        for p in range(2):
            mine = found[p * lines : (p + 1) * lines]
            labels = mine if labels is None else jnp.where(field == 2 * c + p, mine, labels)
    labels = jnp.broadcast_to(labels, (lines, 128)).astype(BF16)
    out_ref[:, :, 4 * width :] = labels.reshape(lines // 2, 2, 128)
    select = jnp.where(hit & (owner_core == plane % 2), 1.0, 0.0).astype(BF16)
    for copy in copies[1:]:
        copy.wait()
    tokens = held[...].reshape(rows, 2 * width)
    for e in range(2):
        part = tokens[:, e * width : (e + 1) * width]
        packed = jnp.dot(select, part, preferred_element_type=F32).astype(BF16)
        for p in range(2):
            at = (2 * p + e) * width
            out_ref[:, :, at : at + width] = packed[p * lines : (p + 1) * lines].reshape(
                lines // 2, 2, width
            )


def shrink(received_ref, weights, partial_ref, label_ref):
    chips, groups, width = received_ref.shape
    width = (width - 128) // 4
    lines = chips * groups
    parity = lax.axis_index("tensor") % 2
    core = lax.axis_index("dp") % 2

    def part(at):
        return received_ref[:, :, at * width : (at + 1) * width].reshape(lines, width)

    product = None
    for e in range(2):
        mine = lax.dot_general(
            jnp.concatenate([part(e), part(2 + e)], axis=0),
            weights[e][...],
            (((1,), (0,)), ((), ())),
            preferred_element_type=F32,
        )
        product = mine if e == 0 else product + mine
    label = received_ref[:, :, 4 * width :].reshape(lines, 128)
    field = iota((lines, 128), 1) >> 5
    here = [
        jnp.where(field == 2 * parity + p, label.astype(F32), 0.0) for p in range(2)
    ]
    here = jnp.concatenate(here, axis=0)
    here = here + pltpu.roll(here, 64, 1)
    here = here + pltpu.roll(here, 32, 1)
    upper = (iota((2 * lines, 128), 1) >> 6).astype(F32)
    total = jnp.where(here == upper + 1.0, product[:, :128], 0.0)
    total = total + jnp.where(here == upper + 3.0, product[:, 128:], 0.0)
    total = total + pltpu.roll(total, 64, 1)
    packed = jnp.where(upper[:lines] == 0.0, total[:lines], total[lines:]).astype(BF16)
    for peer in range(partial_ref.shape[0]):
        partial_ref[peer] = packed
    out_lines = label_ref.shape[0]
    line = iota((out_lines, lines), 0)
    source = (line >> 3) * 2 + (line & 1)
    take = jnp.where(iota((out_lines, lines), 1) == source, 1.0, 0.0).astype(BF16)
    label = jnp.dot(take, label, preferred_element_type=F32)
    line = iota((out_lines, 128), 0)
    label = over_lanes(jnp.where(iota((out_lines, 128), 1) >> 5 == (line >> 1) & 3, label, 0.0))
    other = (label > 0.0) & ((line >> 2) & 1 != core)
    label_ref[...] = jnp.where(other, label + 4.0, label).astype(BF16)


def shrink_kernel(received_ref, own_ref, first_ref, second_ref, partial_ref, label_ref):
    at_home = lax.axis_index("tensor") % 2 == lax.axis_index("dp") % 2

    @pl.when(at_home)
    def _():
        shrink(received_ref, (own_ref, first_ref), partial_ref, label_ref)

    @pl.when(jnp.logical_not(at_home))
    def _():
        shrink(received_ref, (first_ref, second_ref), partial_ref, label_ref)


def expand_kernel(partial_ref, label_ref, up_own_ref, up_other_ref, out_ref):
    planes, lines, _ = partial_ref.shape
    sums = []
    for q in range(2):
        total = partial_ref[q].astype(F32)
        for peer in range(q + 2, planes, 2):
            total = total + partial_ref[peer].astype(F32)
        sums.append(total.reshape(lines // 8, 8, 128))
    spot = iota(sums[0].shape, 1) >> 1
    by_chip = []
    for chip in range(4):
        out = None
        for field in range(4):
            by = 2 * (field - chip) % 8
            piece = pltpu.roll(sums[field // 2], by, 1) if by else sums[field // 2]
            out = piece if field == 0 else jnp.where(spot == field, piece, out)
        by_chip.append(out)
    total = jnp.stack(by_chip, axis=1).reshape(lines * 4, 128)
    upper = iota(total.shape, 1) >> 6
    place = (iota(total.shape, 0) >> 1) & 1
    row = jnp.where(upper == place, total, pltpu.roll(total, 64, 1))
    label = label_ref[...].astype(F32)
    terms = None
    for up_ref, add in ((up_own_ref, 1.0), (up_other_ref, 5.0)):
        at = upper.astype(F32) + add
        left = jnp.where(label == at, row, 0.0)
        right = jnp.where(label == at + 2.0, row, 0.0)
        wide = jnp.concatenate([left, right], axis=1).astype(BF16)
        mine = jnp.dot(wide, up_ref[...], preferred_element_type=F32)
        terms = mine if terms is None else terms + mine
    out_ref[...] = terms.astype(BF16)


def place_kernel(owned, index_ref, out_ref):
    key, place, owner_core, _ = read_index(index_ref, owned)
    rows = key.shape[1]
    target = (key >> 1) * 8 + owner_core * 4 + place * 2 + (key & 1)
    line, column = iota((rows, rows), 0), iota((rows, rows), 1)
    target = jnp.broadcast_to(target, (rows, rows))
    target = jnp.sum(jnp.where(line == column, target, 0).astype(F32), axis=1, keepdims=True)
    out_ref[...] = jnp.where(iota(out_ref.shape, 1).astype(F32) == target, 1.0, 0.0).astype(BF16)


def add_kernel(place_ref, arrived_ref, base_ref, out_ref):
    terms = jnp.dot(place_ref[...], arrived_ref[...], preferred_element_type=F32)
    out_ref[...] = (base_ref[...] + terms).astype(BF16)


def call(kernel, shapes, ins, scratch=(), in_hbm=(), vmem=40):
    nbytes = sum(v.size * v.dtype.itemsize for v in ins)

    def spec(hbm):
        return pl.BlockSpec(memory_space=pltpu.HBM if hbm else pltpu.VMEM)

    return pl.pallas_call(
        kernel,
        out_shape=shapes,
        in_specs=[spec(i in in_hbm) for i in range(len(ins))],
        out_specs=[spec(False) for _ in shapes],
        scratch_shapes=scratch,
        compiler_params=pltpu.CompilerParams(vmem_limit_bytes=vmem * MIB),
        cost_estimate=pl.CostEstimate(flops=0, bytes_accessed=nbytes, transcendentals=0),
    )(*ins)


def on_device(tokens, value_matrix, down, up, index):
    groups, rows_local, features = tokens.shape
    owners = lax.axis_size("dp")
    planes = lax.axis_size("tensor")
    owned, width, rank = down.shape
    columns = up.shape[2]
    rows = groups * rows_local
    shape = jax.ShapeDtypeStruct

    cores = 2
    same_core = [list(range(core, owners, cores)) for core in range(cores)]

    (packed,) = call(
        functools.partial(pack_kernel, owned, planes),
        [shape((owners // cores, groups, 4 * width + 128), BF16)],
        (index, tokens),
        [
            pltpu.VMEM((groups, rows_local, 2 * width), BF16),
            pltpu.VMEM(index.shape, I32),
            pltpu.SemaphoreType.DMA((3,)),
        ],
        in_hbm=(0, 1),
        vmem=62,
    )
    received = lax.all_to_all(
        packed, "dp", split_axis=0, concat_axis=0, tiled=True, axis_index_groups=same_core
    )

    up_own = up.reshape(owned * rank, columns)
    down_later, up_later, _ = lax.optimization_barrier((down, up_own, packed))
    down_own = down_later.transpose(1, 0, 2).reshape(width, owned * rank)
    first, second = [], []
    for i in range(owners):
        for t in range(planes):
            here, other = i * planes, (i ^ 1) * planes
            if i % cores == t % 2:
                first.append((here + t, other + t))
            else:
                first.append((here + t, here + (t - 1) % planes))
                second.append((here + t, other + (t + 1) % planes))
    down_first = lax.ppermute(down_own, ("dp", "tensor"), first)
    down_second = lax.ppermute(down_own, ("dp", "tensor"), second)
    up_other = lax.ppermute(up_later, "dp", [(i, i ^ 1) for i in range(owners)])

    base = jnp.dot(tokens.reshape(rows, features), value_matrix, preferred_element_type=F32)
    (place,) = call(
        functools.partial(place_kernel, owned), [shape((rows, owners * 4), BF16)], (index,)
    )
    received, down_first, down_second, up_other, base, place = lax.optimization_barrier(
        (received, down_first, down_second, up_other, base, place)
    )
    partial, label = call(
        shrink_kernel,
        [shape((planes, owners, 128), BF16), shape((owners * 4, 128), BF16)],
        (received, down_own, down_first, down_second),
    )
    partials = lax.all_to_all(partial, "tensor", split_axis=0, concat_axis=0, tiled=True)
    (terms,) = call(
        expand_kernel,
        [shape((owners * 4, columns), BF16)],
        (partials, label, up_own, up_other),
    )
    arrived = lax.all_to_all(
        terms.reshape(owners // cores, 4 * cores, columns),
        "dp",
        split_axis=0,
        concat_axis=0,
        tiled=True,
        axis_index_groups=same_core,
    ).reshape(owners * 4, columns)
    (out,) = call(add_kernel, [shape((rows, columns), BF16)], (place, arrived, base))
    return out.reshape(groups, rows_local, columns)


def solution(mesh):
    in_specs = (
        P(None, "dp", None),
        P(None, "tensor"),
        P("dp", "tensor", None),
        P("dp", None, "tensor"),
        P(None, "dp"),
    )
    out_specs = P(None, "dp", "tensor")
    return jax.shard_map(
        on_device, mesh=mesh, in_specs=in_specs, out_specs=out_specs, check_vma=False
    )
```
